32 devices in a mesh: depth: 8 (over y, x, core), lat: 4 (over z).
Axes of the slice: x: 2, y: 2, z: 4, core: 2. Of those that a mesh axis runs over, the one named last changes fastest.
Arguments:
- rhs_field: float32 [2, 16, 8, 4096], P(None, 'depth', None, 'lat'), may hold values from -4 to 4
- src_cell: int32 [8], replicated, may hold values from 0 to 4095
- src_layer: int32 [8], replicated, may hold values from 0 to 15
- factor: float32 [16, 32, 3, 2, 128, 128], P('depth', 'lat'), as said below
- couple: float32 [2, 2, 16, 4096], P(None, None, 'depth', 'lat')
Outputs:
- waves: float32 [2, 16, 8, 4096], P(None, 'depth', None, 'lat')
- field: float32 [2, 16, 8, 4096], P(None, 'depth', None, 'lat')
The draws below stay inside these ranges and needn't reach their ends.
Inputs may be any that keep to these rules, and one draw needn't show every extreme that they name: The centre block of every factor is a complex diagonal of modulus 0.92 plus independent entries; the others are independent entries.
All inputs are finite; a program needn't handle non-finite values.
Results may differ from the reference program's by a relative error of at most 0.0003.
Values sent between devices are 32-bit elements; how exact they have to be, the bound alone decides.
A program may use at most 128 MiB of HBM per device.

```python
import math
import jax
import jax.numpy as jnp
from jax import lax

TILE = 128
SHOTS = 8
LAYERS = 16
TILES = 32
LATERAL = 4096


def draw_factor(key, part):
    key_one = jax.random.fold_in(key, 11)
    key_two = jax.random.fold_in(key, 12)
    shape = (LAYERS, TILES, 3, 2, TILE, TILE)
    sigma = math.sqrt(0.16 / (6.0 * TILE))
    random_part = jax.random.normal(key_one, shape, jnp.float32) * sigma
    phase_angle = jax.random.uniform(key_two, (LAYERS, TILES, 1, 1, TILE, 1), jnp.float32, -math.pi, math.pi)
    row_ids = jnp.arange(TILE, dtype=jnp.int32)
    unit_diag = (row_ids[:, None] == row_ids[None, :]).astype(jnp.float32).reshape(1, 1, 1, 1, TILE, TILE)
    centre_flag = (jnp.arange(3, dtype=jnp.int32) == 1).astype(jnp.float32).reshape(1, 1, 3, 1, 1, 1)
    part_flag = jnp.arange(2, dtype=jnp.int32).reshape(1, 1, 1, 2, 1, 1)
    rotation = jnp.where(part_flag == 0, jnp.cos(phase_angle), jnp.sin(phase_angle))
    return random_part + 0.92 * unit_diag * centre_flag * rotation


def draw_couple(key, part):
    key_one = jax.random.fold_in(key, 21)
    key_two = jax.random.fold_in(key, 22)
    shape = (2, 1, LAYERS, LATERAL)
    modulus = jax.random.uniform(key_one, shape, jnp.float32, 0.9, 1.0)
    phase_angle = jax.random.uniform(key_two, shape, jnp.float32, -math.pi, math.pi)
    return jnp.concatenate([modulus * jnp.cos(phase_angle), modulus * jnp.sin(phase_angle)], axis=1)


def with_ends(entries, own_key, least, largest):
    spot = [jax.random.randint(jax.random.fold_in(own_key, axis), (), 0, length) for axis, length in enumerate(entries.shape)]
    widest = entries.shape.index(max(entries.shape))
    neighbour = spot[:widest] + [(spot[widest] + 1) % entries.shape[widest]] + spot[widest + 1:]
    return entries.at[tuple(spot)].set(least).at[tuple(neighbour)].set(largest)


def level_of(key, shape, shards, low, high):
    gain, own = 1.0, jax.random.fold_in(key, 6)
    for dim, blocks in shards:
        draws = jnp.exp(jax.random.uniform(jax.random.fold_in(own, dim), (blocks,), jnp.float32, low / len(shards), high / len(shards)))
        gain = gain * jnp.repeat(draws, shape[dim] // blocks).reshape([-1 if axis == dim else 1 for axis in range(len(shape))])
    return gain


def noise(key, dims, scale, most, cuts=(), held_as=jnp.bfloat16):
    array = jax.random.normal(key, dims, jnp.float32) * scale
    if len(cuts) > 0:
        array = level_of(key, dims, cuts, -0.22, 0.18) * array
    return jnp.clip(array, min=-most, max=most).astype(held_as)


def setup_inputs(seed: int = 0) -> dict:
    key_list = jax.random.split(jax.random.key(seed), 6)
    rhs_field = noise(key_list[0], (2, LAYERS, SHOTS, LATERAL), 0.5, 4.0, ((1, 8), (3, 4)), jnp.float32)
    src_cell = with_ends(jax.random.randint(key_list[1], (SHOTS,), 0, LATERAL), jax.random.fold_in(key_list[1], 1), 0, LATERAL - 1).astype(jnp.int32)
    src_layer = with_ends(jax.random.randint(key_list[2], (SHOTS,), 0, LAYERS), jax.random.fold_in(key_list[2], 1), 0, LAYERS - 1).astype(jnp.int32)
    factor = draw_factor(jax.random.fold_in(key_list[5], 71), 0)
    couple = draw_couple(jax.random.fold_in(key_list[5], 71), 0)
    return dict(rhs_field=rhs_field, src_cell=src_cell, src_layer=src_layer, factor=factor, couple=couple)


def complex_scale(coef, vector):
    real_part = coef[0][None, :] * vector[0] - coef[1][None, :] * vector[1]
    imag_part = coef[0][None, :] * vector[1] + coef[1][None, :] * vector[0]
    return jnp.stack([real_part, imag_part])


def apply_blocks(vector, blocks):
    tile_cells = blocks.shape[-1]
    line_cells = vector.shape[-1]
    tile_count = line_cells // tile_cells
    shot_count = vector.shape[1]
    padded = jnp.pad(vector, ((0, 0), (0, 0), (tile_cells, tile_cells)))
    shifted = jnp.stack([padded[:, :, offset * tile_cells: offset * tile_cells + line_cells].reshape(2, shot_count, tile_count, tile_cells) for offset in range(3)], axis=3)
    form = "stjp,tjpq->stq"
    high = lax.Precision.HIGHEST
    real_out = jnp.einsum(form, shifted[0], blocks[:, :, 0], precision=high) - jnp.einsum(form, shifted[1], blocks[:, :, 1], precision=high)
    imag_out = jnp.einsum(form, shifted[0], blocks[:, :, 1], precision=high) + jnp.einsum(form, shifted[1], blocks[:, :, 0], precision=high)
    return jnp.stack([real_out, imag_out]).reshape(2, shot_count, line_cells)


def reference(rhs_field, src_cell, src_layer, factor, couple):
    layer_ids = jnp.arange(LAYERS, dtype=jnp.int32)
    cell_ids = jnp.arange(LATERAL, dtype=jnp.int32)
    hit = (src_layer[None, :, None] == layer_ids[:, None, None]) & (src_cell[None, :, None] == cell_ids[None, None, :])
    real_part = rhs_field[0] + 4.0 * hit.astype(jnp.float32)
    forcing = jnp.stack([real_part, rhs_field[1]])
    layer_forcing = jnp.moveaxis(forcing, 1, 0)
    couple_down = jnp.moveaxis(couple[0], 1, 0)
    couple_up = jnp.moveaxis(couple[1], 1, 0)

    def down_step(carried, inputs):
        source, blocks, coef = inputs
        new_wave = apply_blocks(source + complex_scale(coef, carried), blocks)
        return new_wave, new_wave

    start_wave = jnp.zeros((2, SHOTS, LATERAL), jnp.float32)
    _, wave_layers = lax.scan(down_step, start_wave, (layer_forcing, factor, couple_down))

    def up_step(carried, inputs):
        wave, blocks, coef = inputs
        new_field = wave + apply_blocks(complex_scale(coef, carried), blocks)
        return new_field, new_field

    _, field_layers = lax.scan(up_step, start_wave, (wave_layers, factor, couple_up), reverse=True)
    return jnp.moveaxis(wave_layers, 0, 1), jnp.moveaxis(field_layers, 0, 1)
```

```python
import functools
import jax
import jax.numpy as jnp
from jax import lax
from jax.experimental import pallas as pl
from jax.experimental.pallas import tpu as pltpu
from jax.sharding import PartitionSpec as P

F32 = jnp.float32
BF16 = jnp.bfloat16
MESH = pl.DeviceIdType.MESH
DOWN, UP = 0, 1
CENTRE, LEFT, RIGHT = 0, 1, 2


def split(value):
    high = value.astype(BF16)
    low = (value - high.astype(F32)).astype(BF16)
    return high, low


def kernel(
    depth_count, lat_count, cell_ref, layer_ref, rhs_ref, couple_ref, factor_ref,
    waves_ref, field_ref,
    raw, weights, edge_raw, edge_weights, rhs_halo, couple_halo,
    forcing0, forcing1, coef, source, inner, main_in, left_in, right_in,
    extra_left, extra_right, out_ext,
    load_sem, halo_send, halo_recv, edge_send, edge_recv, hop_send, hop_recv,
):
    tiles = factor_ref.shape[1]
    tile = factor_ref.shape[-1]
    cells = rhs_ref.shape[-1]
    shots = rhs_ref.shape[2]
    wide = cells + 2 * tile
    d = lax.axis_index("depth")
    l = lax.axis_index("lat")
    has_left, has_right = l > 0, l < lat_count - 1
    has_above, has_below = d > 0, d < depth_count - 1

    def load(layer, t):
        return pltpu.make_async_copy(factor_ref.at[layer, t], raw.at[layer, t], load_sem.at[layer, t])

    for layer in range(2):
        for t in range(tiles):
            load(layer, t).start()

    main_in[...] = jnp.zeros_like(main_in)
    left_in[...] = jnp.zeros_like(left_in)
    right_in[...] = jnp.zeros_like(right_in)
    extra_left[...] = jnp.zeros_like(extra_left)
    extra_right[...] = jnp.zeros_like(extra_right)
    rhs_halo[...] = jnp.zeros_like(rhs_halo)
    couple_halo[...] = jnp.zeros_like(couple_halo)

    @pl.when(l == 0)
    def _():
        edge_raw[:, 0] = jnp.zeros_like(edge_raw[:, 0])

    @pl.when(l == lat_count - 1)
    def _():
        edge_raw[:, 1] = jnp.zeros_like(edge_raw[:, 1])

    barrier = pltpu.get_barrier_semaphore()
    steps = [(a, b) for a in (-1, 0, 1) for b in (-1, 0, 1) if (a, b) != (0, 0)]

    def reachable(a, b):
        return (d + a >= 0) & (d + a < depth_count) & (l + b >= 0) & (l + b < lat_count)

    for a, b in steps:
        @pl.when(reachable(a, b))
        def _():
            pl.semaphore_signal(barrier, inc=1, device_id=(d + a, l + b), device_id_type=MESH)
    rows = 1 + has_above.astype(jnp.int32) + has_below.astype(jnp.int32)
    columns = 1 + has_left.astype(jnp.int32) + has_right.astype(jnp.int32)
    pl.semaphore_wait(barrier, rows * columns - 1)

    def rhs_copy(side):
        cut = pl.ds(cells - tile, tile) if side == 0 else pl.ds(0, tile)
        to = (d, l + 1) if side == 0 else (d, l - 1)
        return pltpu.make_async_remote_copy(
            src_ref=rhs_ref.at[:, 0, :, cut], dst_ref=rhs_halo.at[side],
            send_sem=halo_send.at[0, side], recv_sem=halo_recv.at[0, side],
            device_id=to, device_id_type=MESH)

    def couple_copy(side):
        cut = pl.ds(cells - tile, tile) if side == 0 else pl.ds(0, tile)
        to = (d, l + 1) if side == 0 else (d, l - 1)
        return pltpu.make_async_remote_copy(
            src_ref=couple_ref.at[:, :, :, cut], dst_ref=couple_halo.at[side],
            send_sem=halo_send.at[1, side], recv_sem=halo_recv.at[1, side],
            device_id=to, device_id_type=MESH)

    def edge_copy(layer, side):
        t, j = (tiles - 1, 2) if side == 0 else (0, 0)
        to = (d, l + 1) if side == 0 else (d, l - 1)
        return pltpu.make_async_remote_copy(
            src_ref=factor_ref.at[layer, t, j], dst_ref=edge_raw.at[layer, side],
            send_sem=edge_send.at[layer, side], recv_sem=edge_recv.at[layer, side],
            device_id=to, device_id_type=MESH)

    def sends(side):
        return has_right if side == 0 else has_left

    def receives(side):
        return has_left if side == 0 else has_right

    def hop_copies(way):
        step = 1 if way == DOWN else -1
        onward = has_below if way == DOWN else has_above
        behind = has_above if way == DOWN else has_below
        made = []
        for num, (src, dst, to, go, come) in enumerate((
            (out_ext.at[way, :, :, pl.ds(cells, 2 * tile)], left_in.at[way], (d + step, l + 1),
             onward & has_right, behind & has_left),
            (out_ext.at[way, :, :, pl.ds(0, 2 * tile)], right_in.at[way], (d + step, l - 1),
             onward & has_left, behind & has_right),
            (out_ext.at[way], main_in.at[way], (d + step, l), onward, behind),
            (out_ext.at[way, :, :, pl.ds(cells + tile, tile)], extra_left.at[way], (d, l + 1),
             has_right, has_left),
            (out_ext.at[way, :, :, pl.ds(0, tile)], extra_right.at[way], (d, l - 1),
             has_left, has_right),
        )):
            made.append((pltpu.make_async_remote_copy(
                src_ref=src, dst_ref=dst, send_sem=hop_send.at[way, num], recv_sem=hop_recv.at[way, num],
                device_id=to, device_id_type=MESH), go, come))
        return made

    for side in range(2):
        @pl.when(sends(side))
        def _():
            rhs_copy(side).start()
            couple_copy(side).start()
    for layer in (1, 0):
        for side in range(2):
            @pl.when(sends(side))
            def _():
                edge_copy(layer, side).start()

    def convert(layer):
        def body(t, carry):
            load(layer, t).wait()
            for j in range(3):
                for c in range(2):
                    high, low = split(raw[layer, t, j, c])
                    weights[layer, t, pl.ds(j * tile, tile), pl.ds(c * tile, tile)] = high
                    weights[layer, t, pl.ds((3 + j) * tile, tile), pl.ds(c * tile, tile)] = low
            return carry
        lax.fori_loop(0, tiles, body, 0)

    def convert_edge(layer):
        for side in range(2):
            @pl.when(receives(side))
            def _():
                edge_copy(layer, side).wait_recv()
            for c in range(2):
                high, low = split(edge_raw[layer, side, c])
                edge_weights[layer, side, pl.ds(0, tile), pl.ds(c * tile, tile)] = high
                edge_weights[layer, side, pl.ds(tile, tile), pl.ds(c * tile, tile)] = low

    convert(0)
    convert(1)

    row = lax.broadcasted_iota(jnp.int32, (shots, tile), 0)
    lane = lax.broadcasted_iota(jnp.int32, (shots, tile), 1)
    src_cell = jnp.zeros((shots, tile), jnp.int32)
    src_layer = jnp.zeros((shots, tile), jnp.int32)
    for s in range(shots):
        src_cell = jnp.where(row == s, cell_ref[s], src_cell)
        src_layer = jnp.where(row == s, layer_ref[s], src_layer)

    def pulse(layer, block):
        hit = (src_layer == d * 2 + layer) & (src_cell == l * cells + block * tile + lane)
        return jnp.where(hit, 4.0, 0.0).astype(F32)

    for side in range(2):
        @pl.when(receives(side))
        def _():
            rhs_copy(side).wait_recv()
            couple_copy(side).wait_recv()
        block = -1 if side == 0 else tiles
        at = pl.ds((block + 1) * tile, tile)
        forcing0[0, :, at] = rhs_halo[side, 0] + pulse(0, block)
        forcing0[1, :, at] = rhs_halo[side, 1]
        for c in range(2):
            coef[DOWN, c, :, at] = jnp.broadcast_to(couple_halo[side, DOWN, c, 0:1, :], (shots, tile))
            coef[UP, c, :, at] = jnp.broadcast_to(couple_halo[side, UP, c, 1:2, :], (shots, tile))
    for block in range(tiles):
        at = pl.ds(block * tile, tile)
        to = pl.ds((block + 1) * tile, tile)
        forcing0[0, :, to] = rhs_ref[0, 0, :, at] + pulse(0, block)
        forcing0[1, :, to] = rhs_ref[1, 0, :, at]
        forcing1[0, :, at] = rhs_ref[0, 1, :, at] + pulse(1, block)
        forcing1[1, :, at] = rhs_ref[1, 1, :, at]
        for c in range(2):
            coef[DOWN, c, :, to] = jnp.broadcast_to(couple_ref[DOWN, c, 0:1, at], (shots, tile))
            coef[UP, c, :, to] = jnp.broadcast_to(couple_ref[UP, c, 1:2, at], (shots, tile))
    convert_edge(1)

    def put(target, at, real_part, imag_part):
        for c, value in enumerate((real_part, imag_part)):
            high, low = split(value)
            target[pl.ds(c * shots, shots), at] = high
            target[pl.ds((2 + c) * shots, shots), at] = low

    def product(left_side, right_side):
        both = jnp.dot(left_side, right_side, preferred_element_type=F32)
        both = both[: 2 * shots] + both[2 * shots:]
        real_part = both[:shots, :tile] - both[shots:, tile:]
        imag_part = both[:shots, tile:] + both[shots:, :tile]
        return real_part, imag_part

    def row_block(from_ref, layer, t):
        value = from_ref[:, pl.ds(t * tile, 3 * tile)]
        return product(jnp.concatenate([value, value], axis=1), weights[layer, t])

    def edge_block(from_ref, layer, side):
        block = 0 if side == 0 else tiles - 1
        value = from_ref[:, pl.ds((block + 1) * tile, tile)]
        return product(jnp.concatenate([value, value], axis=1), edge_weights[layer, side])

    def arrived(way, block):
        at = pl.ds((block + 1) * tile, tile)
        parts = []
        for c in range(2):
            value = main_in[way, c, :, at]
            if block <= 0:
                value = value + left_in[way, c, :, pl.ds((block + 1) * tile, tile)]
            if block >= tiles - 1:
                value = value + right_in[way, c, :, pl.ds((block - tiles + 1) * tile, tile)]
            parts.append(value)
        return parts

    zero16 = jnp.zeros((4 * shots, tile), BF16)
    inner[:, pl.ds(0, tile)] = zero16
    inner[:, pl.ds(cells + tile, tile)] = zero16

    def column_step(way, layer, base):
        for side in range(2):
            block = -1 if side == 0 else tiles
            at = pl.ds((block + 1) * tile, tile)
            real_part, imag_part = edge_block(inner, layer, side)
            out_ext[way, 0, :, at] = real_part
            out_ext[way, 1, :, at] = imag_part
        copies = hop_copies(way)
        order = [0, tiles - 1] + list(range(1, tiles - 1))
        for t in order:
            real_part, imag_part = row_block(inner, layer, t)
            if base is not None:
                real_part = real_part + base[0, layer, :, pl.ds(t * tile, tile)]
                imag_part = imag_part + base[1, layer, :, pl.ds(t * tile, tile)]
            at = pl.ds((t + 1) * tile, tile)
            out_ext[way, 0, :, at] = real_part
            out_ext[way, 1, :, at] = imag_part
            if t == tiles - 1:
                for copy, go, _ in copies[:2]:
                    pl.when(go)(copy.start)
        for copy, go, _ in copies[2:]:
            pl.when(go)(copy.start)

    def await_hop(way, first, last):
        for copy, _, come in hop_copies(way)[first:last]:
            pl.when(come)(copy.wait_recv)

    def total(way, result, layer):
        await_hop(way, 3, 5)
        for c in range(2):
            result[c, layer] = out_ext[way, c, :, pl.ds(tile, cells)]
            low, high = pl.ds(0, tile), pl.ds(cells - tile, tile)
            result[c, layer, :, low] = out_ext[way, c, :, pl.ds(tile, tile)] + extra_left[way, c]
            result[c, layer, :, high] = out_ext[way, c, :, pl.ds(cells, tile)] + extra_right[way, c]

    await_hop(DOWN, 0, 3)
    for block in range(-1, tiles + 1):
        at = pl.ds((block + 1) * tile, tile)
        real_in, imag_in = arrived(DOWN, block)
        real_coef, imag_coef = coef[DOWN, 0, :, at], coef[DOWN, 1, :, at]
        put(source, at,
            forcing0[0, :, at] + real_coef * real_in - imag_coef * imag_in,
            forcing0[1, :, at] + real_coef * imag_in + imag_coef * real_in)
    for t in range(tiles):
        at = pl.ds(t * tile, tile)
        real_part, imag_part = row_block(source, 0, t)
        waves_ref[0, 0, :, at] = real_part
        waves_ref[1, 0, :, at] = imag_part
        real_coef, imag_coef = couple_ref[DOWN, 0, 1:2, at], couple_ref[DOWN, 1, 1:2, at]
        put(inner, pl.ds((t + 1) * tile, tile),
            forcing1[0, :, at] + real_coef * real_part - imag_coef * imag_part,
            forcing1[1, :, at] + real_coef * imag_part + imag_coef * real_part)
    column_step(DOWN, 1, None)
    convert_edge(0)
    total(DOWN, waves_ref, 1)

    @pl.when(d == depth_count - 1)
    def _():
        field_ref[:, 1] = waves_ref[:, 1]

    @pl.when(has_below)
    def _():
        await_hop(UP, 0, 3)
        for block in range(-1, tiles + 1):
            at = pl.ds((block + 1) * tile, tile)
            real_in, imag_in = arrived(UP, block)
            real_coef, imag_coef = coef[UP, 0, :, at], coef[UP, 1, :, at]
            put(source, at,
                real_coef * real_in - imag_coef * imag_in,
                real_coef * imag_in + imag_coef * real_in)
        for t in range(tiles):
            at = pl.ds(t * tile, tile)
            real_part, imag_part = row_block(source, 1, t)
            field_ref[0, 1, :, at] = waves_ref[0, 1, :, at] + real_part
            field_ref[1, 1, :, at] = waves_ref[1, 1, :, at] + imag_part

    for t in range(tiles):
        at = pl.ds(t * tile, tile)
        real_part, imag_part = field_ref[0, 1, :, at], field_ref[1, 1, :, at]
        real_coef, imag_coef = couple_ref[UP, 0, 0:1, at], couple_ref[UP, 1, 0:1, at]
        put(inner, pl.ds((t + 1) * tile, tile),
            real_coef * real_part - imag_coef * imag_part,
            real_coef * imag_part + imag_coef * real_part)
    column_step(UP, 0, waves_ref)
    total(UP, field_ref, 0)

    for side in range(2):
        @pl.when(sends(side))
        def _():
            rhs_copy(side).wait_send()
            couple_copy(side).wait_send()
            edge_copy(0, side).wait_send()
            edge_copy(1, side).wait_send()
    for way in (DOWN, UP):
        for copy, go, _ in hop_copies(way):
            pl.when(go)(copy.wait_send)


def shards(depth_count, lat_count, rhs_field, src_cell, src_layer, factor, couple):
    layers, tiles = factor.shape[:2]
    tile = factor.shape[-1]
    shots, cells = rhs_field.shape[2:]
    assert layers == 2 and cells == tiles * tile
    wide = cells + 2 * tile
    vmem, smem = pl.BlockSpec(memory_space=pltpu.VMEM), pl.BlockSpec(memory_space=pltpu.SMEM)
    dma = pltpu.SemaphoreType.DMA
    return pl.pallas_call(
        functools.partial(kernel, depth_count, lat_count),
        out_shape=[jax.ShapeDtypeStruct(rhs_field.shape, F32)] * 2,
        in_specs=[smem, smem, vmem, vmem, pl.BlockSpec(memory_space=pl.ANY)],
        out_specs=[vmem, vmem],
        scratch_shapes=[
            pltpu.VMEM(factor.shape, F32),
            pltpu.VMEM((2, tiles, 6 * tile, 2 * tile), BF16),
            pltpu.VMEM((2, 2, 2, tile, tile), F32),
            pltpu.VMEM((2, 2, 2 * tile, 2 * tile), BF16),
            pltpu.VMEM((2, 2, shots, tile), F32),
            pltpu.VMEM((2, 2, 2, 2, tile), F32),
            pltpu.VMEM((2, shots, wide), F32),
            pltpu.VMEM((2, shots, cells), F32),
            pltpu.VMEM((2, 2, shots, wide), F32),
            pltpu.VMEM((4 * shots, wide), BF16),
            pltpu.VMEM((4 * shots, wide), BF16),
            pltpu.VMEM((2, 2, shots, wide), F32),
            pltpu.VMEM((2, 2, shots, 2 * tile), F32),
            pltpu.VMEM((2, 2, shots, 2 * tile), F32),
            pltpu.VMEM((2, 2, shots, tile), F32),
            pltpu.VMEM((2, 2, shots, tile), F32),
            pltpu.VMEM((2, 2, shots, wide), F32),
            dma((2, tiles)), dma((2, 2)), dma((2, 2)), dma((2, 2)), dma((2, 2)), dma((2, 5)), dma((2, 5)),
        ],
        compiler_params=pltpu.CompilerParams(
            collective_id=0, has_side_effects=True, vmem_limit_bytes=40 * 1024 * 1024),
        name="sweeps",
    )(src_cell, src_layer, rhs_field, couple, factor)


def solution(mesh):
    placed = (
        P(None, "depth", None, "lat"),
        P(),
        P(),
        P("depth", "lat", None, None, None, None),
        P(None, None, "depth", "lat"),
    )
    return jax.shard_map(
        functools.partial(shards, mesh.shape["depth"], mesh.shape["lat"]),
        mesh=mesh,
        in_specs=placed,
        out_specs=(P(None, "depth", None, "lat"), P(None, "depth", None, "lat")),
        check_vma=False,
    )
```

```python
import functools
import jax
import jax.numpy as jnp
from jax import lax
from jax.experimental import pallas as pl
from jax.experimental.pallas import tpu as pltpu
from jax.sharding import PartitionSpec as P

F32 = jnp.float32
BF16 = jnp.bfloat16
MESH = pl.DeviceIdType.MESH
DOWN, UP = 0, 1
CENTRE, LEFT, RIGHT = 0, 1, 2


def split(value):
    high = value.astype(BF16)
    low = (value - high.astype(F32)).astype(BF16)
    return high, low


def kernel(
    depth_count, lat_count, cell_hbm, layer_hbm, rhs_hbm, couple_hbm, factor_ref,
    waves_ref, field_ref,
    cell_ref, layer_ref, rhs_ref, couple_ref, raw, weights, edge_raw, edge_weights, rhs_halo, couple_halo,
    forcing0, forcing1, coef, source, inner, main_in, left_in, right_in,
    extra_left, extra_right, out_ext,
    small_sem, load_sem, halo_send, halo_recv, edge_send, edge_recv, hop_send, hop_recv,
):
    tiles = factor_ref.shape[1]
    tile = factor_ref.shape[-1]
    cells = rhs_hbm.shape[-1]
    shots = rhs_hbm.shape[2]
    wide = cells + 2 * tile
    d = lax.axis_index("depth")
    l = lax.axis_index("lat")
    has_left, has_right = l > 0, l < lat_count - 1
    has_above, has_below = d > 0, d < depth_count - 1

    def load(layer, t):
        return pltpu.make_async_copy(factor_ref.at[layer, t], raw.at[layer, t], load_sem.at[layer, t])

    small = [
        pltpu.make_async_copy(src, dst, small_sem.at[num])
        for num, (src, dst) in enumerate((
            (rhs_hbm, rhs_ref), (couple_hbm, couple_ref), (cell_hbm, cell_ref), (layer_hbm, layer_ref)))
    ]
    for copy in small:
        copy.start()
    for layer in range(2):
        for t in range(tiles):
            load(layer, t).start()

    main_in[...] = jnp.zeros_like(main_in)
    left_in[...] = jnp.zeros_like(left_in)
    right_in[...] = jnp.zeros_like(right_in)
    extra_left[...] = jnp.zeros_like(extra_left)
    extra_right[...] = jnp.zeros_like(extra_right)
    rhs_halo[...] = jnp.zeros_like(rhs_halo)
    couple_halo[...] = jnp.zeros_like(couple_halo)

    @pl.when(l == 0)
    def _():
        edge_raw[:, 0] = jnp.zeros_like(edge_raw[:, 0])

    @pl.when(l == lat_count - 1)
    def _():
        edge_raw[:, 1] = jnp.zeros_like(edge_raw[:, 1])

    barrier = pltpu.get_barrier_semaphore()
    steps = [(a, b) for a in (-1, 0, 1) for b in (-1, 0, 1) if (a, b) != (0, 0)]

    def reachable(a, b):
        return (d + a >= 0) & (d + a < depth_count) & (l + b >= 0) & (l + b < lat_count)

    for a, b in steps:
        @pl.when(reachable(a, b))
        def _():
            pl.semaphore_signal(barrier, inc=1, device_id=(d + a, l + b), device_id_type=MESH)
    rows = 1 + has_above.astype(jnp.int32) + has_below.astype(jnp.int32)
    columns = 1 + has_left.astype(jnp.int32) + has_right.astype(jnp.int32)
    pl.semaphore_wait(barrier, rows * columns - 1)

    def rhs_copy(side):
        cut = pl.ds(cells - tile, tile) if side == 0 else pl.ds(0, tile)
        to = (d, l + 1) if side == 0 else (d, l - 1)
        return pltpu.make_async_remote_copy(
            src_ref=rhs_hbm.at[:, 0, :, cut], dst_ref=rhs_halo.at[side],
            send_sem=halo_send.at[0, side], recv_sem=halo_recv.at[0, side],
            device_id=to, device_id_type=MESH)

    def couple_copy(side):
        cut = pl.ds(cells - tile, tile) if side == 0 else pl.ds(0, tile)
        to = (d, l + 1) if side == 0 else (d, l - 1)
        return pltpu.make_async_remote_copy(
            src_ref=couple_hbm.at[:, :, :, cut], dst_ref=couple_halo.at[side],
            send_sem=halo_send.at[1, side], recv_sem=halo_recv.at[1, side],
            device_id=to, device_id_type=MESH)

    def edge_copy(layer, side):
        t, j = (tiles - 1, 2) if side == 0 else (0, 0)
        to = (d, l + 1) if side == 0 else (d, l - 1)
        return pltpu.make_async_remote_copy(
            src_ref=factor_ref.at[layer, t, j], dst_ref=edge_raw.at[layer, side],
            send_sem=edge_send.at[layer, side], recv_sem=edge_recv.at[layer, side],
            device_id=to, device_id_type=MESH)

    def sends(side):
        return has_right if side == 0 else has_left

    def receives(side):
        return has_left if side == 0 else has_right

    def hop_copies(way):
        step = 1 if way == DOWN else -1
        onward = has_below if way == DOWN else has_above
        behind = has_above if way == DOWN else has_below
        made = []
        blocks = tiles + 2
        middle = blocks // 2
        chunks = [(0, 2), (blocks - 2, blocks), (2, middle), (middle, blocks - 2)]
        for num, (src, dst, to, go, come) in enumerate((
            (out_ext.at[way, :, :, pl.ds(0, 2 * tile)], right_in.at[way], (d + step, l - 1),
             onward & has_left, behind & has_right),
            (out_ext.at[way, :, :, pl.ds(cells, 2 * tile)], left_in.at[way], (d + step, l + 1),
             onward & has_right, behind & has_left),
            *((out_ext.at[way, :, :, pl.ds(first * tile, (last - first) * tile)],
               main_in.at[way, :, :, pl.ds(first * tile, (last - first) * tile)],
               (d + step, l), onward, behind) for first, last in chunks),
            (out_ext.at[way, :, :, pl.ds(cells + tile, tile)], extra_left.at[way], (d, l + 1),
             has_right, has_left),
            (out_ext.at[way, :, :, pl.ds(0, tile)], extra_right.at[way], (d, l - 1),
             has_left, has_right),
        )):
            made.append((pltpu.make_async_remote_copy(
                src_ref=src, dst_ref=dst, send_sem=hop_send.at[way, num], recv_sem=hop_recv.at[way, num],
                device_id=to, device_id_type=MESH), go, come))
        return made

    for side in range(2):
        @pl.when(sends(side))
        def _():
            rhs_copy(side).start()
            couple_copy(side).start()
    for layer in (1, 0):
        for side in range(2):
            @pl.when(sends(side))
            def _():
                edge_copy(layer, side).start()

    def convert(layer):
        def body(t, carry):
            load(layer, t).wait()
            for j in range(3):
                for c in range(2):
                    high, low = split(raw[layer, t, j, c])
                    weights[layer, t, pl.ds(j * tile, tile), pl.ds(c * tile, tile)] = high
                    weights[layer, t, pl.ds((3 + j) * tile, tile), pl.ds(c * tile, tile)] = low
            return carry
        lax.fori_loop(0, tiles, body, 0)

    def convert_edge(layer):
        for side in range(2):
            @pl.when(receives(side))
            def _():
                edge_copy(layer, side).wait_recv()
            for c in range(2):
                high, low = split(edge_raw[layer, side, c])
                edge_weights[layer, side, pl.ds(0, tile), pl.ds(c * tile, tile)] = high
                edge_weights[layer, side, pl.ds(tile, tile), pl.ds(c * tile, tile)] = low

    convert(0)
    convert(1)

    for copy in small:
        copy.wait()

    row = lax.broadcasted_iota(jnp.int32, (shots, tile), 0)
    lane = lax.broadcasted_iota(jnp.int32, (shots, tile), 1)
    src_cell = jnp.zeros((shots, tile), jnp.int32)
    src_layer = jnp.zeros((shots, tile), jnp.int32)
    for s in range(shots):
        src_cell = jnp.where(row == s, cell_ref[s], src_cell)
        src_layer = jnp.where(row == s, layer_ref[s], src_layer)

    def pulse(layer, block):
        hit = (src_layer == d * 2 + layer) & (src_cell == l * cells + block * tile + lane)
        return jnp.where(hit, 4.0, 0.0).astype(F32)

    for side in range(2):
        @pl.when(receives(side))
        def _():
            rhs_copy(side).wait_recv()
            couple_copy(side).wait_recv()
        block = -1 if side == 0 else tiles
        at = pl.ds((block + 1) * tile, tile)
        forcing0[0, :, at] = rhs_halo[side, 0] + pulse(0, block)
        forcing0[1, :, at] = rhs_halo[side, 1]
        for c in range(2):
            coef[DOWN, c, :, at] = jnp.broadcast_to(couple_halo[side, DOWN, c, 0:1, :], (shots, tile))
            coef[UP, c, :, at] = jnp.broadcast_to(couple_halo[side, UP, c, 1:2, :], (shots, tile))
    for block in range(tiles):
        at = pl.ds(block * tile, tile)
        to = pl.ds((block + 1) * tile, tile)
        forcing0[0, :, to] = rhs_ref[0, 0, :, at] + pulse(0, block)
        forcing0[1, :, to] = rhs_ref[1, 0, :, at]
        forcing1[0, :, at] = rhs_ref[0, 1, :, at] + pulse(1, block)
        forcing1[1, :, at] = rhs_ref[1, 1, :, at]
        for c in range(2):
            coef[DOWN, c, :, to] = jnp.broadcast_to(couple_ref[DOWN, c, 0:1, at], (shots, tile))
            coef[UP, c, :, to] = jnp.broadcast_to(couple_ref[UP, c, 1:2, at], (shots, tile))
    convert_edge(1)

    def put(target, at, real_part, imag_part):
        for c, value in enumerate((real_part, imag_part)):
            high, low = split(value)
            target[pl.ds(c * shots, shots), at] = high
            target[pl.ds((2 + c) * shots, shots), at] = low

    def product(left_side, right_side):
        both = jnp.dot(left_side, right_side, preferred_element_type=F32)
        both = both[: 2 * shots] + both[2 * shots:]
        real_part = both[:shots, :tile] - both[shots:, tile:]
        imag_part = both[:shots, tile:] + both[shots:, :tile]
        return real_part, imag_part

    def row_block(from_ref, layer, t):
        value = from_ref[:, pl.ds(t * tile, 3 * tile)]
        return product(jnp.concatenate([value, value], axis=1), weights[layer, t])

    def edge_block(from_ref, layer, side):
        block = 0 if side == 0 else tiles - 1
        value = from_ref[:, pl.ds((block + 1) * tile, tile)]
        return product(jnp.concatenate([value, value], axis=1), edge_weights[layer, side])

    def arrived(way, block):
        at = pl.ds((block + 1) * tile, tile)
        parts = []
        for c in range(2):
            value = main_in[way, c, :, at]
            if block <= 0:
                value = value + left_in[way, c, :, pl.ds((block + 1) * tile, tile)]
            if block >= tiles - 1:
                value = value + right_in[way, c, :, pl.ds((block - tiles + 1) * tile, tile)]
            parts.append(value)
        return parts

    zero16 = jnp.zeros((4 * shots, tile), BF16)
    inner[:, pl.ds(0, tile)] = zero16
    inner[:, pl.ds(cells + tile, tile)] = zero16

    def column_step(way, layer, base):
        for side in range(2):
            block = -1 if side == 0 else tiles
            at = pl.ds((block + 1) * tile, tile)
            real_part, imag_part = edge_block(inner, layer, side)
            out_ext[way, 0, :, at] = real_part
            out_ext[way, 1, :, at] = imag_part
        copies = hop_copies(way)
        order = [0, tiles - 1] + list(range(1, tiles - 1))
        for t in order:
            real_part, imag_part = row_block(inner, layer, t)
            if base is not None:
                real_part = real_part + base[0, layer, :, pl.ds(t * tile, tile)]
                imag_part = imag_part + base[1, layer, :, pl.ds(t * tile, tile)]
            at = pl.ds((t + 1) * tile, tile)
            out_ext[way, 0, :, at] = real_part
            out_ext[way, 1, :, at] = imag_part
            starts = {0: (0, 2), tiles - 1: (1, 3), tiles // 2 - 1: (4,), tiles - 2: (5, 6, 7)}
            for num in starts.get(t, ()):
                copy, go, _ = copies[num]
                pl.when(go)(copy.start)

    def await_hop(way, first, last):
        for copy, _, come in hop_copies(way)[first:last]:
            pl.when(come)(copy.wait_recv)

    def total(way, result, layer):
        await_hop(way, 6, 8)
        for c in range(2):
            result[c, layer] = out_ext[way, c, :, pl.ds(tile, cells)]
            low, high = pl.ds(0, tile), pl.ds(cells - tile, tile)
            result[c, layer, :, low] = out_ext[way, c, :, pl.ds(tile, tile)] + extra_left[way, c]
            result[c, layer, :, high] = out_ext[way, c, :, pl.ds(cells, tile)] + extra_right[way, c]

    await_hop(DOWN, 0, 6)
    for block in range(-1, tiles + 1):
        at = pl.ds((block + 1) * tile, tile)
        real_in, imag_in = arrived(DOWN, block)
        real_coef, imag_coef = coef[DOWN, 0, :, at], coef[DOWN, 1, :, at]
        put(source, at,
            forcing0[0, :, at] + real_coef * real_in - imag_coef * imag_in,
            forcing0[1, :, at] + real_coef * imag_in + imag_coef * real_in)
    for t in range(tiles):
        at = pl.ds(t * tile, tile)
        real_part, imag_part = row_block(source, 0, t)
        waves_ref[0, 0, :, at] = real_part
        waves_ref[1, 0, :, at] = imag_part
        real_coef, imag_coef = couple_ref[DOWN, 0, 1:2, at], couple_ref[DOWN, 1, 1:2, at]
        put(inner, pl.ds((t + 1) * tile, tile),
            forcing1[0, :, at] + real_coef * real_part - imag_coef * imag_part,
            forcing1[1, :, at] + real_coef * imag_part + imag_coef * real_part)
    column_step(DOWN, 1, None)
    convert_edge(0)
    total(DOWN, waves_ref, 1)

    @pl.when(d == depth_count - 1)
    def _():
        field_ref[:, 1] = waves_ref[:, 1]

    @pl.when(has_below)
    def _():
        await_hop(UP, 0, 6)
        for block in range(-1, tiles + 1):
            at = pl.ds((block + 1) * tile, tile)
            real_in, imag_in = arrived(UP, block)
            real_coef, imag_coef = coef[UP, 0, :, at], coef[UP, 1, :, at]
            put(source, at,
                real_coef * real_in - imag_coef * imag_in,
                real_coef * imag_in + imag_coef * real_in)
        for t in range(tiles):
            at = pl.ds(t * tile, tile)
            real_part, imag_part = row_block(source, 1, t)
            field_ref[0, 1, :, at] = waves_ref[0, 1, :, at] + real_part
            field_ref[1, 1, :, at] = waves_ref[1, 1, :, at] + imag_part

    for t in range(tiles):
        at = pl.ds(t * tile, tile)
        real_part, imag_part = field_ref[0, 1, :, at], field_ref[1, 1, :, at]
        real_coef, imag_coef = couple_ref[UP, 0, 0:1, at], couple_ref[UP, 1, 0:1, at]
        put(inner, pl.ds((t + 1) * tile, tile),
            real_coef * real_part - imag_coef * imag_part,
            real_coef * imag_part + imag_coef * real_part)
    column_step(UP, 0, waves_ref)
    total(UP, field_ref, 0)

    for side in range(2):
        @pl.when(sends(side))
        def _():
            rhs_copy(side).wait_send()
            couple_copy(side).wait_send()
            edge_copy(0, side).wait_send()
            edge_copy(1, side).wait_send()
    for way in (DOWN, UP):
        for copy, go, _ in hop_copies(way):
            pl.when(go)(copy.wait_send)


def shards(depth_count, lat_count, rhs_field, src_cell, src_layer, factor, couple):
    layers, tiles = factor.shape[:2]
    tile = factor.shape[-1]
    shots, cells = rhs_field.shape[2:]
    assert layers == 2 and cells == tiles * tile
    wide = cells + 2 * tile
    vmem = pl.BlockSpec(memory_space=pltpu.VMEM)
    dma = pltpu.SemaphoreType.DMA
    return pl.pallas_call(
        functools.partial(kernel, depth_count, lat_count),
        out_shape=[jax.ShapeDtypeStruct(rhs_field.shape, F32)] * 2,
        in_specs=[pl.BlockSpec(memory_space=pltpu.HBM)] * 5,
        out_specs=[vmem, vmem],
        scratch_shapes=[
            pltpu.SMEM(src_cell.shape, jnp.int32),
            pltpu.SMEM(src_layer.shape, jnp.int32),
            pltpu.VMEM(rhs_field.shape, F32),
            pltpu.VMEM(couple.shape, F32),
            pltpu.VMEM(factor.shape, F32),
            pltpu.VMEM((2, tiles, 6 * tile, 2 * tile), BF16),
            pltpu.VMEM((2, 2, 2, tile, tile), F32),
            pltpu.VMEM((2, 2, 2 * tile, 2 * tile), BF16),
            pltpu.VMEM((2, 2, shots, tile), F32),
            pltpu.VMEM((2, 2, 2, 2, tile), F32),
            pltpu.VMEM((2, shots, wide), F32),
            pltpu.VMEM((2, shots, cells), F32),
            pltpu.VMEM((2, 2, shots, wide), F32),
            pltpu.VMEM((4 * shots, wide), BF16),
            pltpu.VMEM((4 * shots, wide), BF16),
            pltpu.VMEM((2, 2, shots, wide), F32),
            pltpu.VMEM((2, 2, shots, 2 * tile), F32),
            pltpu.VMEM((2, 2, shots, 2 * tile), F32),
            pltpu.VMEM((2, 2, shots, tile), F32),
            pltpu.VMEM((2, 2, shots, tile), F32),
            pltpu.VMEM((2, 2, shots, wide), F32),
            dma((4,)), dma((2, tiles)), dma((2, 2)), dma((2, 2)), dma((2, 2)), dma((2, 2)), dma((2, 8)), dma((2, 8)),
        ],
        compiler_params=pltpu.CompilerParams(
            collective_id=0, has_side_effects=True, vmem_limit_bytes=63 * 1024 * 1024),
        name="sweeps",
    )(src_cell, src_layer, rhs_field, couple, factor)


def solution(mesh):
    placed = (
        P(None, "depth", None, "lat"),
        P(),
        P(),
        P("depth", "lat", None, None, None, None),
        P(None, None, "depth", "lat"),
    )
    return jax.shard_map(
        functools.partial(shards, mesh.shape["depth"], mesh.shape["lat"]),
        mesh=mesh,
        in_specs=placed,
        out_specs=(P(None, "depth", None, "lat"), P(None, "depth", None, "lat")),
        check_vma=False,
    )
```

```python
import functools
import jax
import jax.numpy as jnp
from jax import lax
from jax.experimental import pallas as pl
from jax.experimental.pallas import tpu as pltpu
from jax.sharding import PartitionSpec as P

F32 = jnp.float32
BF16 = jnp.bfloat16
MESH = pl.DeviceIdType.MESH
DOWN, UP = 0, 1
CENTRE, LEFT, RIGHT = 0, 1, 2


def split(value):
    high = value.astype(BF16)
    low = (value - high.astype(F32)).astype(BF16)
    return high, low


def kernel(
    depth_count, lat_count, cell_hbm, layer_hbm, rhs_hbm, couple_hbm, factor_ref,
    waves_ref, field_ref,
    cell_ref, layer_ref, rhs, couple, raw, weights, edge_raw, edge_weights,
    source, inner, out_ext, main_in, left_in, right_in, side_left, side_right,
    extra_left, extra_right, waves, field, result_in,
    small_sem, self_sem, load_sem, part_send, part_recv, mid_send, mid_recv, mid_self,
    edge_send, edge_recv, strip_send, strip_recv, halo_send, halo_recv,
    hop_send, hop_recv, side_send, side_recv, result_send, result_recv,
):
    tile = factor_ref.shape[-1]
    tiles = factor_ref.shape[1] // 2
    cells = tiles * tile
    shots = rhs_hbm.shape[2]
    wide = cells + 2 * tile
    d = lax.axis_index("depth")
    l = lax.axis_index("lat")
    core = lax.rem(d, 2)
    other = 1 - core
    pair = lax.div(d, 2)
    half = 2 * l + core
    pairs, halves = depth_count // 2, 2 * lat_count
    has_left, has_right = half > 0, half < halves - 1
    has_above, has_below = pair > 0, pair < pairs - 1
    partner = (2 * pair + other, l)

    def place(pair_step, half_step):
        spot = half + half_step
        return (2 * (pair + pair_step) + lax.rem(spot + 2, 2), lax.div(spot + 2, 2) - 1)

    def remote(src, dst, send_sem, recv_sem, to):
        return pltpu.make_async_remote_copy(
            src_ref=src, dst_ref=dst, send_sem=send_sem, recv_sem=recv_sem,
            device_id=to, device_id_type=MESH)

    def load(i, t):
        return pltpu.make_async_copy(
            factor_ref.at[i, core * tiles + t], raw.at[2 * core + i, t], load_sem.at[i, t])

    def part_out(i, t):
        return remote(factor_ref.at[i, other * tiles + t], raw.at[2 * core + i, t],
                      part_send.at[i, t], part_recv.at[i, t], partner)

    def mid_edge(i, target):
        src = factor_ref.at[i, tiles - target, 2 * target]
        return src, edge_raw.at[2 * core + i, 1 - target]

    def mid_out(i):
        src, dst = mid_edge(i, other)
        return remote(src, dst, mid_send.at[i], mid_recv.at[i], partner)

    def mid_own(i):
        src, dst = mid_edge(i, core)
        return pltpu.make_async_copy(src, dst, mid_self.at[i])

    def beside(side):
        return (2 * pair, l + 1) if side == 0 else (2 * pair + 1, l - 1)

    def edge_out(i, side):
        t, j = (2 * tiles - 1, 2) if side == 0 else (0, 0)
        return remote(factor_ref.at[i, t, j], edge_raw.at[2 * core + i, side],
                      edge_send.at[i, side], edge_recv.at[2 * core + i], beside(side))

    def edge_in(k):
        return remote(edge_raw.at[k, core], edge_raw.at[k, core],
                      edge_send.at[0, 0], edge_recv.at[k], partner)

    def strip_cut(ref, target):
        return ref.at[..., pl.ds(pl.multiple_of(target * (tiles - 1) * tile, tile), cells + tile)]

    def strip_slot(ref, target):
        return ref.at[core, ..., pl.ds(pl.multiple_of((1 - target) * tile, tile), cells + tile)]

    inputs = ((rhs_hbm, rhs), (couple_hbm, couple))

    def strip_out(n):
        src, dst = inputs[n]
        return remote(strip_cut(src, other), strip_slot(dst, other), strip_send.at[n], strip_recv.at[n], partner)

    def strip_own(n):
        src, dst = inputs[n]
        return pltpu.make_async_copy(strip_cut(src, core), strip_slot(dst, core), self_sem.at[n])

    def halo_out(n, side):
        src, dst = inputs[n]
        cut = pl.ds((2 * tiles - 1) * tile, tile) if side == 0 else pl.ds(0, tile)
        slot = pl.ds(0, tile) if side == 0 else pl.ds(cells + tile, tile)
        return remote(src.at[..., cut], dst.at[core, ..., slot],
                      halo_send.at[n, side], halo_recv.at[n, core], beside(side))

    def halo_in(n, owner):
        dst = inputs[n][1]
        slot = dst.at[owner, ..., pl.ds(pl.multiple_of(core * (cells + tile), tile), tile)]
        return remote(slot, slot, halo_send.at[n, 0], halo_recv.at[n, owner], partner)

    sends = (l < lat_count - 1, l > 0)
    outer = ((core == 0) & (l > 0)) | ((core == 1) & (l < lat_count - 1))

    small = [pltpu.make_async_copy(cell_hbm, cell_ref, small_sem.at[0]),
             pltpu.make_async_copy(layer_hbm, layer_ref, small_sem.at[1])]
    for copy in small:
        copy.start()
    for n in range(2):
        strip_own(n).start()
    for i in range(2):
        mid_own(i).start()
    for i in range(2):
        for t in range(tiles):
            load(i, t).start()

    for ref in (main_in, left_in, right_in, side_left, side_right, extra_left, extra_right):
        ref[...] = jnp.zeros_like(ref)

    @pl.when(jnp.logical_not(has_left))
    def _():
        edge_raw[:, 0] = jnp.zeros_like(edge_raw[:, 0])
        rhs[..., pl.ds(0, tile)] = jnp.zeros((2, 2, 2, shots, tile), F32)
        couple[..., pl.ds(0, tile)] = jnp.zeros((2, 2, 2, 2, tile), F32)

    @pl.when(jnp.logical_not(has_right))
    def _():
        edge_raw[:, 1] = jnp.zeros_like(edge_raw[:, 1])
        rhs[..., pl.ds(cells + tile, tile)] = jnp.zeros((2, 2, 2, shots, tile), F32)
        couple[..., pl.ds(cells + tile, tile)] = jnp.zeros((2, 2, 2, 2, tile), F32)

    barrier = pltpu.get_barrier_semaphore()
    steps = [(a, b) for a in (-1, 0, 1) for b in (-1, 0, 1) if (a, b) != (0, 0)] + [(0, -2), (0, 2)]
    peers = 0
    for a, b in steps:
        there = (pair + a >= 0) & (pair + a < pairs) & (half + b >= 0) & (half + b < halves)
        peers = peers + there.astype(jnp.int32)

        @pl.when(there)
        def _():
            pl.semaphore_signal(barrier, inc=1, device_id=place(a, b), device_id_type=MESH)
    pl.semaphore_wait(barrier, peers)

    for n in range(2):
        strip_out(n).start()
    for side in range(2):
        @pl.when(sends[side])
        def _():
            for n in range(2):
                halo_out(n, side).start()
    for i in (1, 0):
        mid_out(i).start()
        for side in range(2):
            @pl.when(sends[side])
            def _():
                edge_out(i, side).start()
    for i in range(2):
        for t in range(tiles):
            part_out(i, t).start()

    def convert(k):
        owner, i = k // 2, k % 2

        def step(t, carry):
            @pl.when(core == owner)
            def _():
                load(i, t).wait()

            @pl.when(core != owner)
            def _():
                remote(raw.at[k, t], raw.at[k, t], part_send.at[i, t], part_recv.at[i, t], partner).wait_recv()
            for j in range(3):
                for c in range(2):
                    high, low = split(raw[k, t, j, c])
                    weights[k, t, pl.ds(j * tile, tile), pl.ds(c * tile, tile)] = high
                    weights[k, t, pl.ds((3 + j) * tile, tile), pl.ds(c * tile, tile)] = low
            return carry
        lax.fori_loop(0, tiles, step, 0)

    def convert_edge(k):
        owner, i = k // 2, k % 2

        @pl.when(core == owner)
        def _():
            mid_own(i).wait()

        @pl.when(core != owner)
        def _():
            slot = edge_raw.at[k, other]
            remote(slot, slot, mid_send.at[i], mid_recv.at[i], partner).wait_recv()
        pl.when(outer)(edge_in(k).wait_recv)
        for side in range(2):
            for c in range(2):
                high, low = split(edge_raw[k, side, c])
                edge_weights[k, side, pl.ds(0, tile), pl.ds(c * tile, tile)] = high
                edge_weights[k, side, pl.ds(tile, tile), pl.ds(c * tile, tile)] = low

    convert(0)
    convert(1)
    for copy in small:
        copy.wait()
    for n in range(2):
        strip_own(n).wait()
        src, dst = inputs[n]
        slot = dst.at[other, ..., pl.ds(pl.multiple_of(other * tile, tile), cells + tile)]
        remote(slot, slot, strip_send.at[n], strip_recv.at[n], partner).wait_recv()

        @pl.when(outer)
        def _():
            for owner in range(2):
                halo_in(n, owner).wait_recv()

    row = lax.broadcasted_iota(jnp.int32, (shots, wide), 0)
    lane = lax.broadcasted_iota(jnp.int32, (shots, wide), 1) + (half * cells - tile)
    src_cell = jnp.zeros((shots, wide), jnp.int32)
    src_layer = jnp.zeros((shots, wide), jnp.int32)
    for s in range(shots):
        src_cell = jnp.where(row == s, cell_ref[s], src_cell)
        src_layer = jnp.where(row == s, layer_ref[s], src_layer)
    for k in range(4):
        hit = (src_layer == pair * 4 + k) & (src_cell == lane)
        rhs[k // 2, 0, k % 2] = rhs[k // 2, 0, k % 2] + jnp.where(hit, 4.0, 0.0).astype(F32)
    convert_edge(1)

    def put(target, at, parts):
        for c, value in enumerate(parts):
            high, low = split(value)
            target[pl.ds(c * shots, shots), at] = high
            target[pl.ds((2 + c) * shots, shots), at] = low

    def scaled(way, k, at, parts):
        real_coef = couple[k // 2, way, 0, k % 2:k % 2 + 1, at]
        imag_coef = couple[k // 2, way, 1, k % 2:k % 2 + 1, at]
        real_part = real_coef * parts[0] - imag_coef * parts[1]
        imag_part = real_coef * parts[1] + imag_coef * parts[0]
        if way == DOWN:
            real_part = rhs[k // 2, 0, k % 2, :, at] + real_part
            imag_part = rhs[k // 2, 1, k % 2, :, at] + imag_part
        return real_part, imag_part

    def product(value, right_side):
        both = jnp.dot(jnp.concatenate([value, value], axis=1), right_side, preferred_element_type=F32)
        both = both[: 2 * shots] + both[2 * shots:]
        return (both[:shots, :tile] - both[shots:, tile:], both[:shots, tile:] + both[shots:, :tile])

    def row_block(from_ref, k, t):
        return product(from_ref[:, pl.ds(t * tile, 3 * tile)], weights[k, t])

    def arrived(main, low, high, block):
        at = pl.ds(block * tile, tile)
        parts = []
        for c in range(2):
            value = main[c, :, at]
            if block < 2:
                value = value + low[c, :, at]
            if block >= tiles:
                value = value + high[c, :, pl.ds((block - tiles) * tile, tile)]
            parts.append(value)
        return parts

    blocks = tiles + 2
    chunks = [(0, 2), (blocks - 2, blocks), (2, blocks - 2)]

    def span(first, last):
        return pl.ds(first * tile, (last - first) * tile)

    def side_copies(way):
        out = out_ext.at[2 * way]
        return [
            (remote(out.at[:, :, span(0, 2)], side_right.at[way], side_send.at[way, 0], side_recv.at[way, 0],
                    place(0, -1)), has_left, has_right),
            (remote(out.at[:, :, span(tiles, blocks)], side_left.at[way], side_send.at[way, 1], side_recv.at[way, 1],
                    place(0, 1)), has_right, has_left),
        ]

    def hop_copies(way):
        out = out_ext.at[2 * way + 1]
        step = 1 if way == DOWN else -1
        onward = has_below if way == DOWN else has_above
        behind = has_above if way == DOWN else has_below
        table = [
            (span(0, 2), right_in.at[way], place(step, -1), onward & has_left, behind & has_right),
            (span(tiles, blocks), left_in.at[way], place(step, 1), onward & has_right, behind & has_left),
        ]
        for first, last in chunks:
            table.append((span(first, last), main_in.at[way, :, :, span(first, last)], place(step, 0), onward, behind))
        table.append((span(blocks - 1, blocks), extra_left.at[way], place(0, 1), has_right, has_left))
        table.append((span(0, 1), extra_right.at[way], place(0, -1), has_left, has_right))
        return [
            (remote(out.at[:, :, cut], dst, hop_send.at[way, num], hop_recv.at[way, num], to), go, come)
            for num, (cut, dst, to, go, come) in enumerate(table)
        ]

    zero = jnp.zeros((4 * shots, tile), BF16)
    inner[:, pl.ds(0, tile)] = zero
    inner[:, pl.ds(cells + tile, tile)] = zero

    def column_step(stage, k, base):
        for side in range(2):
            block = 0 if side == 0 else tiles + 1
            own = pl.ds(tile, tile) if side == 0 else pl.ds(cells, tile)
            real_part, imag_part = product(inner[:, own], edge_weights[k, side])
            out_ext[stage, 0, :, pl.ds(block * tile, tile)] = real_part
            out_ext[stage, 1, :, pl.ds(block * tile, tile)] = imag_part
        way = stage // 2
        copies = side_copies(way) if stage % 2 == 0 else hop_copies(way)
        starts = {tiles - 1: (0, 1)} if stage % 2 == 0 else {tiles - 1: (0, 1, 2, 3), tiles - 2: (4, 5, 6)}
        for t in [0, tiles - 1] + list(range(1, tiles - 1)):
            parts = row_block(inner, k, t)
            for c in range(2):
                value = parts[c]
                if base is not None:
                    value = value + base[k, c, :, pl.ds(t * tile, tile)]
                out_ext[stage, c, :, pl.ds((t + 1) * tile, tile)] = value
            for num in starts.get(t, ()):
                copy, go, _ = copies[num]
                pl.when(go)(copy.start)

    def take(copies):
        for copy, _, come in copies:
            pl.when(come)(copy.wait_recv)

    def first_source(way, k, main, low, high, result, result_k):
        for block in range(blocks):
            at = pl.ds(block * tile, tile)
            parts = arrived(main, low, high, block)
            if result is not None and 0 < block <= tiles:
                for c in range(2):
                    result[result_k, c, :, pl.ds((block - 1) * tile, tile)] = parts[c]
            put(source, at, scaled(way, k, at, parts))

    def second_source(way, row_k, k, result, base):
        for t in range(tiles):
            at = pl.ds(t * tile, tile)
            parts = row_block(source, row_k, t)
            if base is not None:
                parts = [parts[c] + base[row_k, c, :, at] for c in range(2)]
            for c in range(2):
                result[row_k, c, :, at] = parts[c]
            to = pl.ds((t + 1) * tile, tile)
            put(inner, to, scaled(way, k, to, parts))

    def total(way, result, k):
        take(hop_copies(way)[5:])
        out = out_ext.at[2 * way + 1]
        for c in range(2):
            for t in range(tiles):
                value = out[c, :, pl.ds((t + 1) * tile, tile)]
                if t == 0:
                    value = value + extra_left[way, c]
                if t == tiles - 1:
                    value = value + extra_right[way, c]
                result[k, c, :, pl.ds(t * tile, tile)] = value

    def second_layers():
        convert(2)
        convert(3)
        convert_edge(3)

    pl.when(has_above)(second_layers)
    take(hop_copies(DOWN)[:5])
    first_source(DOWN, 0, main_in.at[DOWN], left_in.at[DOWN], right_in.at[DOWN], None, 0)
    second_source(DOWN, 0, 1, waves, None)
    column_step(0, 1, None)
    pl.when(jnp.logical_not(has_above))(second_layers)
    take(side_copies(DOWN))
    first_source(DOWN, 2, out_ext.at[0], side_left.at[DOWN], side_right.at[DOWN], waves, 1)
    second_source(DOWN, 2, 3, waves, None)
    column_step(1, 3, None)
    convert_edge(2)
    convert_edge(0)
    total(DOWN, waves, 3)

    def result_copy(n, ref):
        return remote(ref.at[pl.ds(2 * other, 2)], result_in.at[n], result_send.at[n], result_recv.at[n], partner)

    result_copy(0, waves).start()

    @pl.when(jnp.logical_not(has_below))
    def _():
        for t in range(tiles):
            at = pl.ds(t * tile, tile)
            to = pl.ds((t + 1) * tile, tile)
            parts = [waves[3, c, :, at] for c in range(2)]
            for c in range(2):
                field[3, c, :, at] = parts[c]
            put(inner, to, scaled(UP, 2, to, parts))

    @pl.when(has_below)
    def _():
        take(hop_copies(UP)[:5])
        first_source(UP, 3, main_in.at[UP], left_in.at[UP], right_in.at[UP], None, 0)
        second_source(UP, 3, 2, field, waves)

    column_step(2, 2, waves)
    take(side_copies(UP))
    first_source(UP, 1, out_ext.at[2], side_left.at[UP], side_right.at[UP], field, 2)
    second_source(UP, 1, 0, field, waves)
    column_step(3, 0, waves)
    total(UP, field, 0)
    result_copy(1, field).start()

    for n, (ref, out_ref) in enumerate(((waves, waves_ref), (field, field_ref))):
        mine = pl.ds(pl.multiple_of(core * cells, tile), cells)
        theirs = pl.ds(pl.multiple_of(other * cells, tile), cells)
        for i in range(2):
            for c in range(2):
                out_ref[c, i, :, mine] = ref[2 * core + i, c]
        result_copy(n, ref).wait_recv()
        for i in range(2):
            for c in range(2):
                out_ref[c, i, :, theirs] = result_in[n, i, c]

    for n, ref in enumerate((waves, field)):
        result_copy(n, ref).wait_send()
        strip_out(n).wait_send()
    for i in range(2):
        mid_out(i).wait_send()
        for t in range(tiles):
            part_out(i, t).wait_send()
    for side in range(2):
        @pl.when(sends[side])
        def _():
            for n in range(2):
                halo_out(n, side).wait_send()
                edge_out(n, side).wait_send()
    for way in (DOWN, UP):
        for copy, go, _ in side_copies(way) + hop_copies(way):
            pl.when(go)(copy.wait_send)


def shards(depth_count, lat_count, rhs_field, src_cell, src_layer, factor, couple):
    layers, full_tiles = factor.shape[:2]
    tile = factor.shape[-1]
    shots = rhs_field.shape[2]
    assert layers == 2 and full_tiles % 2 == 0 and depth_count % 2 == 0
    tiles = full_tiles // 2
    cells = tiles * tile
    wide = cells + 2 * tile
    vmem = pl.BlockSpec(memory_space=pltpu.VMEM)
    dma = pltpu.SemaphoreType.DMA
    return pl.pallas_call(
        functools.partial(kernel, depth_count, lat_count),
        out_shape=[jax.ShapeDtypeStruct(rhs_field.shape, F32)] * 2,
        in_specs=[pl.BlockSpec(memory_space=pltpu.HBM)] * 5,
        out_specs=[vmem, vmem],
        scratch_shapes=[
            pltpu.SMEM(src_cell.shape, jnp.int32),
            pltpu.SMEM(src_layer.shape, jnp.int32),
            pltpu.VMEM((2, 2, 2, shots, wide), F32),
            pltpu.VMEM((2, 2, 2, 2, wide), F32),
            pltpu.VMEM((4, tiles, 3, 2, tile, tile), F32),
            pltpu.VMEM((4, tiles, 6 * tile, 2 * tile), BF16),
            pltpu.VMEM((4, 2, 2, tile, tile), F32),
            pltpu.VMEM((4, 2, 2 * tile, 2 * tile), BF16),
            pltpu.VMEM((4 * shots, wide), BF16),
            pltpu.VMEM((4 * shots, wide), BF16),
            pltpu.VMEM((4, 2, shots, wide), F32),
            pltpu.VMEM((2, 2, shots, wide), F32),
            *[pltpu.VMEM((2, 2, shots, 2 * tile), F32)] * 4,
            *[pltpu.VMEM((2, 2, shots, tile), F32)] * 2,
            *[pltpu.VMEM((4, 2, shots, cells), F32)] * 2,
            pltpu.VMEM((2, 2, 2, shots, cells), F32),
            dma((2,)), dma((2,)), dma((2, tiles)), dma((2, tiles)), dma((2, tiles)),
            dma((2,)), dma((2,)), dma((2,)),
            dma((2, 2)), dma((4,)), dma((2,)), dma((2,)), dma((2, 2)), dma((2, 2)),
            dma((2, 7)), dma((2, 7)), dma((2, 2)), dma((2, 2)), dma((2,)), dma((2,)),
        ],
        compiler_params=pltpu.CompilerParams(
            collective_id=0, has_side_effects=True, vmem_limit_bytes=63 * 1024 * 1024),
        name="sweeps",
    )(src_cell, src_layer, rhs_field, couple, factor)


def solution(mesh):
    placed = (
        P(None, "depth", None, "lat"),
        P(),
        P(),
        P("depth", "lat", None, None, None, None),
        P(None, None, "depth", "lat"),
    )
    return jax.shard_map(
        functools.partial(shards, mesh.shape["depth"], mesh.shape["lat"]),
        mesh=mesh,
        in_specs=placed,
        out_specs=(P(None, "depth", None, "lat"), P(None, "depth", None, "lat")),
        check_vma=False,
    )
```

```python
import functools
import jax
import jax.numpy as jnp
from jax import lax
from jax.experimental import pallas as pl
from jax.experimental.pallas import tpu as pltpu
from jax.sharding import PartitionSpec as P

F32 = jnp.float32
BF16 = jnp.bfloat16
MESH = pl.DeviceIdType.MESH
DOWN, UP = 0, 1
CENTRE, LEFT, RIGHT = 0, 1, 2


def split(value):
    high = value.astype(BF16)
    low = (value - high.astype(F32)).astype(BF16)
    return high, low


def kernel(
    depth_count, lat_count, cell_hbm, layer_hbm, rhs_hbm, couple_hbm, factor_ref,
    waves_ref, field_ref,
    cell_ref, layer_ref, rhs, couple, raw, weights, edge_raw, edge_weights,
    source, inner, out_ext, main_in, left_in, right_in, side_left, side_right,
    extra_left, extra_right, waves, field, result_in,
    small_sem, self_sem, load_sem, part_send, part_recv, mid_send, mid_recv, mid_self,
    edge_send, edge_recv, strip_send, strip_recv, halo_send, halo_recv,
    hop_send, hop_recv, side_send, side_recv, result_send, result_recv,
):
    tile = factor_ref.shape[-1]
    tiles = factor_ref.shape[1] // 2
    cells = tiles * tile
    shots = rhs_hbm.shape[2]
    wide = cells + 2 * tile
    d = lax.axis_index("depth")
    l = lax.axis_index("lat")
    core = lax.rem(d, 2)
    other = 1 - core
    pair = lax.div(d, 2)
    half = 2 * l + core
    pairs, halves = depth_count // 2, 2 * lat_count
    has_left, has_right = half > 0, half < halves - 1
    has_above, has_below = pair > 0, pair < pairs - 1
    partner = (2 * pair + other, l)

    def place(pair_step, half_step):
        spot = half + half_step
        return (2 * (pair + pair_step) + lax.rem(spot + 2, 2), lax.div(spot + 2, 2) - 1)

    def remote(src, dst, send_sem, recv_sem, to):
        return pltpu.make_async_remote_copy(
            src_ref=src, dst_ref=dst, send_sem=send_sem, recv_sem=recv_sem,
            device_id=to, device_id_type=MESH)

    def load(i, t):
        return pltpu.make_async_copy(
            factor_ref.at[i, core * tiles + t], raw.at[2 * core + i, t], load_sem.at[i, t])

    def part_out(i, t):
        return remote(factor_ref.at[i, other * tiles + t], raw.at[2 * core + i, t],
                      part_send.at[i, t], part_recv.at[i, t], partner)

    def mid_edge(i, target):
        src = factor_ref.at[i, tiles - target, 2 * target]
        return src, edge_raw.at[2 * core + i, 1 - target]

    def mid_out(i):
        src, dst = mid_edge(i, other)
        return remote(src, dst, mid_send.at[i], mid_recv.at[i], partner)

    def mid_own(i):
        src, dst = mid_edge(i, core)
        return pltpu.make_async_copy(src, dst, mid_self.at[i])

    def beside(side):
        return (2 * pair, l + 1) if side == 0 else (2 * pair + 1, l - 1)

    def edge_out(i, side):
        t, j = (2 * tiles - 1, 2) if side == 0 else (0, 0)
        return remote(factor_ref.at[i, t, j], edge_raw.at[2 * core + i, side],
                      edge_send.at[i, side], edge_recv.at[2 * core + i], beside(side))

    def edge_in(k):
        return remote(edge_raw.at[k, core], edge_raw.at[k, core],
                      edge_send.at[0, 0], edge_recv.at[k], partner)

    def strip_cut(ref, target):
        return ref.at[..., pl.ds(pl.multiple_of(target * (tiles - 1) * tile, tile), cells + tile)]

    def strip_slot(ref, target):
        return ref.at[core, ..., pl.ds(pl.multiple_of((1 - target) * tile, tile), cells + tile)]

    inputs = ((rhs_hbm, rhs), (couple_hbm, couple))

    def strip_out(n):
        src, dst = inputs[n]
        return remote(strip_cut(src, other), strip_slot(dst, other), strip_send.at[n], strip_recv.at[n], partner)

    def strip_own(n):
        src, dst = inputs[n]
        return pltpu.make_async_copy(strip_cut(src, core), strip_slot(dst, core), self_sem.at[n])

    def halo_out(n, side):
        src, dst = inputs[n]
        cut = pl.ds((2 * tiles - 1) * tile, tile) if side == 0 else pl.ds(0, tile)
        slot = pl.ds(0, tile) if side == 0 else pl.ds(cells + tile, tile)
        return remote(src.at[..., cut], dst.at[core, ..., slot],
                      halo_send.at[n, side], halo_recv.at[n, core], beside(side))

    def halo_in(n, owner):
        dst = inputs[n][1]
        slot = dst.at[owner, ..., pl.ds(pl.multiple_of(core * (cells + tile), tile), tile)]
        return remote(slot, slot, halo_send.at[n, 0], halo_recv.at[n, owner], partner)

    sends = (l < lat_count - 1, l > 0)
    outer = ((core == 0) & (l > 0)) | ((core == 1) & (l < lat_count - 1))

    small = [pltpu.make_async_copy(cell_hbm, cell_ref, small_sem.at[0]),
             pltpu.make_async_copy(layer_hbm, layer_ref, small_sem.at[1])]
    for copy in small:
        copy.start()
    for n in range(2):
        strip_own(n).start()
    for i in range(2):
        mid_own(i).start()
    for i in range(2):
        for t in range(tiles):
            load(i, t).start()

    for ref in (main_in, left_in, right_in, side_left, side_right, extra_left, extra_right):
        ref[...] = jnp.zeros_like(ref)

    @pl.when(jnp.logical_not(has_left))
    def _():
        edge_raw[:, 0] = jnp.zeros_like(edge_raw[:, 0])
        rhs[..., pl.ds(0, tile)] = jnp.zeros((2, 2, 2, shots, tile), F32)
        couple[..., pl.ds(0, tile)] = jnp.zeros((2, 2, 2, 2, tile), F32)

    @pl.when(jnp.logical_not(has_right))
    def _():
        edge_raw[:, 1] = jnp.zeros_like(edge_raw[:, 1])
        rhs[..., pl.ds(cells + tile, tile)] = jnp.zeros((2, 2, 2, shots, tile), F32)
        couple[..., pl.ds(cells + tile, tile)] = jnp.zeros((2, 2, 2, 2, tile), F32)

    barrier = pltpu.get_barrier_semaphore()
    steps = [(a, b) for a in (-1, 0, 1) for b in (-1, 0, 1) if (a, b) != (0, 0)] + [(0, -2), (0, 2)]
    peers = 0
    for a, b in steps:
        there = (pair + a >= 0) & (pair + a < pairs) & (half + b >= 0) & (half + b < halves)
        peers = peers + there.astype(jnp.int32)

        @pl.when(there)
        def _():
            pl.semaphore_signal(barrier, inc=1, device_id=place(a, b), device_id_type=MESH)
    pl.semaphore_wait(barrier, peers)

    for n in range(2):
        strip_out(n).start()
    for side in range(2):
        @pl.when(sends[side])
        def _():
            for n in range(2):
                halo_out(n, side).start()
    for i in (1, 0):
        mid_out(i).start()
        for side in range(2):
            @pl.when(sends[side])
            def _():
                edge_out(i, side).start()
    for i in range(2):
        for t in range(tiles):
            part_out(i, t).start()

    def convert(k):
        owner, i = k // 2, k % 2

        def step(t, carry):
            @pl.when(core == owner)
            def _():
                load(i, t).wait()

            @pl.when(core != owner)
            def _():
                remote(raw.at[k, t], raw.at[k, t], part_send.at[i, t], part_recv.at[i, t], partner).wait_recv()
            for j in range(3):
                for c in range(2):
                    high, low = split(raw[k, t, j, c])
                    weights[k, t, pl.ds(j * tile, tile), pl.ds(c * tile, tile)] = high
                    weights[k, t, pl.ds((3 + j) * tile, tile), pl.ds(c * tile, tile)] = low
            return carry
        lax.fori_loop(0, tiles, step, 0)

    def convert_edge(k):
        owner, i = k // 2, k % 2

        @pl.when(core == owner)
        def _():
            mid_own(i).wait()

        @pl.when(core != owner)
        def _():
            slot = edge_raw.at[k, other]
            remote(slot, slot, mid_send.at[i], mid_recv.at[i], partner).wait_recv()
        pl.when(outer)(edge_in(k).wait_recv)
        for side in range(2):
            for c in range(2):
                high, low = split(edge_raw[k, side, c])
                edge_weights[k, side, pl.ds(0, tile), pl.ds(c * tile, tile)] = high
                edge_weights[k, side, pl.ds(tile, tile), pl.ds(c * tile, tile)] = low

    convert(0)
    convert(1)
    for copy in small:
        copy.wait()
    for n in range(2):
        strip_own(n).wait()
        src, dst = inputs[n]
        slot = dst.at[other, ..., pl.ds(pl.multiple_of(other * tile, tile), cells + tile)]
        remote(slot, slot, strip_send.at[n], strip_recv.at[n], partner).wait_recv()

        @pl.when(outer)
        def _():
            for owner in range(2):
                halo_in(n, owner).wait_recv()

    row = lax.broadcasted_iota(jnp.int32, (shots, wide), 0)
    lane = lax.broadcasted_iota(jnp.int32, (shots, wide), 1) + (half * cells - tile)
    src_cell = jnp.zeros((shots, wide), jnp.int32)
    src_layer = jnp.zeros((shots, wide), jnp.int32)
    for s in range(shots):
        src_cell = jnp.where(row == s, cell_ref[s], src_cell)
        src_layer = jnp.where(row == s, layer_ref[s], src_layer)
    for k in range(4):
        hit = (src_layer == pair * 4 + k) & (src_cell == lane)
        rhs[k // 2, 0, k % 2] = rhs[k // 2, 0, k % 2] + jnp.where(hit, 4.0, 0.0).astype(F32)
    convert_edge(1)

    def put(target, at, parts):
        high, low = split(jnp.concatenate(parts, axis=0))
        target[pl.ds(0, 2 * shots), at] = high
        target[pl.ds(2 * shots, 2 * shots), at] = low

    def scaled(way, k, at, parts):
        real_coef = couple[k // 2, way, 0, k % 2:k % 2 + 1, at]
        imag_coef = couple[k // 2, way, 1, k % 2:k % 2 + 1, at]
        real_part = real_coef * parts[0] - imag_coef * parts[1]
        imag_part = real_coef * parts[1] + imag_coef * parts[0]
        if way == DOWN:
            real_part = rhs[k // 2, 0, k % 2, :, at] + real_part
            imag_part = rhs[k // 2, 1, k % 2, :, at] + imag_part
        return real_part, imag_part

    def product(value, right_side):
        both = jnp.dot(jnp.concatenate([value, value], axis=1), right_side, preferred_element_type=F32)
        both = both[: 2 * shots] + both[2 * shots:]
        return (both[:shots, :tile] - both[shots:, tile:], both[:shots, tile:] + both[shots:, :tile])

    def row_block(from_ref, k, t):
        return product(from_ref[:, pl.ds(t * tile, 3 * tile)], weights[k, t])

    def arrived(main, low, high, block):
        at = pl.ds(block * tile, tile)
        parts = []
        for c in range(2):
            value = main[c, :, at]
            if block < 2:
                value = value + low[c, :, at]
            if block >= tiles:
                value = value + high[c, :, pl.ds((block - tiles) * tile, tile)]
            parts.append(value)
        return parts

    blocks = tiles + 2
    chunks = [(0, 2), (blocks - 2, blocks), (2, blocks - 2)]

    def span(first, last):
        return pl.ds(first * tile, (last - first) * tile)

    def side_copies(way):
        out = out_ext.at[2 * way]
        return [
            (remote(out.at[:, :, span(0, 2)], side_right.at[way], side_send.at[way, 0], side_recv.at[way, 0],
                    place(0, -1)), has_left, has_right),
            (remote(out.at[:, :, span(tiles, blocks)], side_left.at[way], side_send.at[way, 1], side_recv.at[way, 1],
                    place(0, 1)), has_right, has_left),
        ]

    def hop_copies(way):
        out = out_ext.at[2 * way + 1]
        step = 1 if way == DOWN else -1
        onward = has_below if way == DOWN else has_above
        behind = has_above if way == DOWN else has_below
        table = [
            (span(0, 2), right_in.at[way], place(step, -1), onward & has_left, behind & has_right),
            (span(tiles, blocks), left_in.at[way], place(step, 1), onward & has_right, behind & has_left),
        ]
        for first, last in chunks:
            table.append((span(first, last), main_in.at[way, :, :, span(first, last)], place(step, 0), onward, behind))
        table.append((span(blocks - 1, blocks), extra_left.at[way], place(0, 1), has_right, has_left))
        table.append((span(0, 1), extra_right.at[way], place(0, -1), has_left, has_right))
        return [
            (remote(out.at[:, :, cut], dst, hop_send.at[way, num], hop_recv.at[way, num], to), go, come)
            for num, (cut, dst, to, go, come) in enumerate(table)
        ]

    zero = jnp.zeros((4 * shots, tile), BF16)
    inner[:, pl.ds(0, tile)] = zero
    inner[:, pl.ds(cells + tile, tile)] = zero

    def column_step(stage, k, base):
        for side in range(2):
            block = 0 if side == 0 else tiles + 1
            own = pl.ds(tile, tile) if side == 0 else pl.ds(cells, tile)
            real_part, imag_part = product(inner[:, own], edge_weights[k, side])
            out_ext[stage, 0, :, pl.ds(block * tile, tile)] = real_part
            out_ext[stage, 1, :, pl.ds(block * tile, tile)] = imag_part
        way = stage // 2
        copies = side_copies(way) if stage % 2 == 0 else hop_copies(way)
        starts = {tiles - 1: (0, 1)} if stage % 2 == 0 else {tiles - 1: (0, 1, 2, 3), tiles - 2: (4, 5, 6)}
        for t in [0, tiles - 1] + list(range(1, tiles - 1)):
            parts = row_block(inner, k, t)
            for c in range(2):
                value = parts[c]
                if base is not None:
                    value = value + base[k, c, :, pl.ds(t * tile, tile)]
                out_ext[stage, c, :, pl.ds((t + 1) * tile, tile)] = value
            for num in starts.get(t, ()):
                copy, go, _ = copies[num]
                pl.when(go)(copy.start)

    def take(copies):
        for copy, _, come in copies:
            pl.when(come)(copy.wait_recv)

    def first_source(way, k, main, low, high, result, result_k):
        for block in range(blocks):
            at = pl.ds(block * tile, tile)
            parts = arrived(main, low, high, block)
            if result is not None and 0 < block <= tiles:
                for c in range(2):
                    result[result_k, c, :, pl.ds((block - 1) * tile, tile)] = parts[c]
            put(source, at, scaled(way, k, at, parts))

    def second_source(way, row_k, k, result, base):
        for t in range(tiles):
            at = pl.ds(t * tile, tile)
            parts = row_block(source, row_k, t)
            if base is not None:
                parts = [parts[c] + base[row_k, c, :, at] for c in range(2)]
            for c in range(2):
                result[row_k, c, :, at] = parts[c]
            to = pl.ds((t + 1) * tile, tile)
            put(inner, to, scaled(way, k, to, parts))

    def total(way, result, k):
        take(hop_copies(way)[5:])
        out = out_ext.at[2 * way + 1]
        for c in range(2):
            for t in range(tiles):
                value = out[c, :, pl.ds((t + 1) * tile, tile)]
                if t == 0:
                    value = value + extra_left[way, c]
                if t == tiles - 1:
                    value = value + extra_right[way, c]
                result[k, c, :, pl.ds(t * tile, tile)] = value

    def second_layers():
        convert(2)
        convert(3)
        convert_edge(3)

    pl.when(has_above)(second_layers)
    take(hop_copies(DOWN)[:5])
    first_source(DOWN, 0, main_in.at[DOWN], left_in.at[DOWN], right_in.at[DOWN], None, 0)
    second_source(DOWN, 0, 1, waves, None)
    column_step(0, 1, None)
    pl.when(jnp.logical_not(has_above))(second_layers)
    take(side_copies(DOWN))
    first_source(DOWN, 2, out_ext.at[0], side_left.at[DOWN], side_right.at[DOWN], waves, 1)
    second_source(DOWN, 2, 3, waves, None)
    column_step(1, 3, None)
    convert_edge(2)
    convert_edge(0)
    total(DOWN, waves, 3)

    def result_copy(n, ref):
        return remote(ref.at[pl.ds(2 * other, 2)], result_in.at[n], result_send.at[n], result_recv.at[n], partner)

    result_copy(0, waves).start()

    @pl.when(jnp.logical_not(has_below))
    def _():
        for t in range(tiles):
            at = pl.ds(t * tile, tile)
            to = pl.ds((t + 1) * tile, tile)
            parts = [waves[3, c, :, at] for c in range(2)]
            for c in range(2):
                field[3, c, :, at] = parts[c]
            put(inner, to, scaled(UP, 2, to, parts))

    @pl.when(has_below)
    def _():
        take(hop_copies(UP)[:5])
        first_source(UP, 3, main_in.at[UP], left_in.at[UP], right_in.at[UP], None, 0)
        second_source(UP, 3, 2, field, waves)

    column_step(2, 2, waves)
    take(side_copies(UP))
    first_source(UP, 1, out_ext.at[2], side_left.at[UP], side_right.at[UP], field, 2)
    second_source(UP, 1, 0, field, waves)
    column_step(3, 0, waves)
    total(UP, field, 0)
    result_copy(1, field).start()

    for n, (ref, out_ref) in enumerate(((waves, waves_ref), (field, field_ref))):
        mine = pl.ds(pl.multiple_of(core * cells, tile), cells)
        theirs = pl.ds(pl.multiple_of(other * cells, tile), cells)
        for i in range(2):
            for c in range(2):
                out_ref[c, i, :, mine] = ref[2 * core + i, c]
        result_copy(n, ref).wait_recv()
        for i in range(2):
            for c in range(2):
                out_ref[c, i, :, theirs] = result_in[n, i, c]

    for n, ref in enumerate((waves, field)):
        result_copy(n, ref).wait_send()
        strip_out(n).wait_send()
    for i in range(2):
        mid_out(i).wait_send()
        for t in range(tiles):
            part_out(i, t).wait_send()
    for side in range(2):
        @pl.when(sends[side])
        def _():
            for n in range(2):
                halo_out(n, side).wait_send()
                edge_out(n, side).wait_send()
    for way in (DOWN, UP):
        for copy, go, _ in side_copies(way) + hop_copies(way):
            pl.when(go)(copy.wait_send)


def shards(depth_count, lat_count, rhs_field, src_cell, src_layer, factor, couple):
    layers, full_tiles = factor.shape[:2]
    tile = factor.shape[-1]
    shots = rhs_field.shape[2]
    assert layers == 2 and full_tiles % 2 == 0 and depth_count % 2 == 0
    tiles = full_tiles // 2
    cells = tiles * tile
    wide = cells + 2 * tile
    vmem = pl.BlockSpec(memory_space=pltpu.VMEM)
    dma = pltpu.SemaphoreType.DMA
    return pl.pallas_call(
        functools.partial(kernel, depth_count, lat_count),
        out_shape=[jax.ShapeDtypeStruct(rhs_field.shape, F32)] * 2,
        in_specs=[pl.BlockSpec(memory_space=pltpu.HBM)] * 5,
        out_specs=[vmem, vmem],
        scratch_shapes=[
            pltpu.SMEM(src_cell.shape, jnp.int32),
            pltpu.SMEM(src_layer.shape, jnp.int32),
            pltpu.VMEM((2, 2, 2, shots, wide), F32),
            pltpu.VMEM((2, 2, 2, 2, wide), F32),
            pltpu.VMEM((4, tiles, 3, 2, tile, tile), F32),
            pltpu.VMEM((4, tiles, 6 * tile, 2 * tile), BF16),
            pltpu.VMEM((4, 2, 2, tile, tile), F32),
            pltpu.VMEM((4, 2, 2 * tile, 2 * tile), BF16),
            pltpu.VMEM((4 * shots, wide), BF16),
            pltpu.VMEM((4 * shots, wide), BF16),
            pltpu.VMEM((4, 2, shots, wide), F32),
            pltpu.VMEM((2, 2, shots, wide), F32),
            *[pltpu.VMEM((2, 2, shots, 2 * tile), F32)] * 4,
            *[pltpu.VMEM((2, 2, shots, tile), F32)] * 2,
            *[pltpu.VMEM((4, 2, shots, cells), F32)] * 2,
            pltpu.VMEM((2, 2, 2, shots, cells), F32),
            dma((2,)), dma((2,)), dma((2, tiles)), dma((2, tiles)), dma((2, tiles)),
            dma((2,)), dma((2,)), dma((2,)),
            dma((2, 2)), dma((4,)), dma((2,)), dma((2,)), dma((2, 2)), dma((2, 2)),
            dma((2, 7)), dma((2, 7)), dma((2, 2)), dma((2, 2)), dma((2,)), dma((2,)),
        ],
        compiler_params=pltpu.CompilerParams(
            collective_id=0, has_side_effects=True, vmem_limit_bytes=44 * 1024 * 1024),
        name="sweeps",
    )(*[pltpu.with_memory_space_constraint(value, pltpu.HBM)
        for value in (src_cell, src_layer, rhs_field, couple, factor)])


def solution(mesh):
    placed = (
        P(None, "depth", None, "lat"),
        P(),
        P(),
        P("depth", "lat", None, None, None, None),
        P(None, None, "depth", "lat"),
    )
    return jax.shard_map(
        functools.partial(shards, mesh.shape["depth"], mesh.shape["lat"]),
        mesh=mesh,
        in_specs=placed,
        out_specs=(P(None, "depth", None, "lat"), P(None, "depth", None, "lat")),
        check_vma=False,
    )
```

```python
import functools
import jax
import jax.numpy as jnp
from jax import lax
from jax.experimental import pallas as pl
from jax.experimental.pallas import tpu as pltpu
from jax.sharding import PartitionSpec as P

F32 = jnp.float32
BF16 = jnp.bfloat16
MESH = pl.DeviceIdType.MESH
DOWN, UP = 0, 1
CENTRE, LEFT, RIGHT = 0, 1, 2


def split(value):
    high = value.astype(BF16)
    low = (value - high.astype(F32)).astype(BF16)
    return high, low


def kernel(
    depth_count, lat_count, cell_hbm, layer_hbm, rhs_hbm, couple_hbm, factor_ref,
    waves_ref, field_ref,
    cell_ref, layer_ref, rhs, couple, raw, weights, edge_raw, edge_weights,
    source, inner, out_ext, main_in, left_in, right_in, side_left, side_right,
    extra_left, extra_right, waves, field, result_in,
    small_sem, self_sem, load_sem, part_send, part_recv, mid_send, mid_recv, mid_self,
    edge_send, edge_recv, strip_send, strip_recv, halo_send, halo_recv,
    hop_send, hop_recv, side_send, side_recv, result_send, result_recv,
):
    tile = factor_ref.shape[-1]
    tiles = factor_ref.shape[1] // 2
    cells = tiles * tile
    shots = rhs_hbm.shape[2]
    wide = cells + 2 * tile
    d = lax.axis_index("depth")
    l = lax.axis_index("lat")
    core = lax.rem(d, 2)
    other = 1 - core
    pair = lax.div(d, 2)
    half = 2 * l + core
    pairs, halves = depth_count // 2, 2 * lat_count
    has_left, has_right = half > 0, half < halves - 1
    has_above, has_below = pair > 0, pair < pairs - 1
    partner = (2 * pair + other, l)

    def place(pair_step, half_step):
        spot = half + half_step
        return (2 * (pair + pair_step) + lax.rem(spot + 2, 2), lax.div(spot + 2, 2) - 1)

    def remote(src, dst, send_sem, recv_sem, to):
        return pltpu.make_async_remote_copy(
            src_ref=src, dst_ref=dst, send_sem=send_sem, recv_sem=recv_sem,
            device_id=to, device_id_type=MESH)

    def load(i, t):
        return pltpu.make_async_copy(
            factor_ref.at[i, core * tiles + t], raw.at[2 * core + i, t], load_sem.at[i, t])

    def part_out(i, t):
        return remote(factor_ref.at[i, other * tiles + t], raw.at[2 * core + i, t],
                      part_send.at[i, t], part_recv.at[i, t], partner)

    def mid_edge(i, target):
        src = factor_ref.at[i, tiles - target, 2 * target]
        return src, edge_raw.at[2 * core + i, 1 - target]

    def mid_out(i):
        src, dst = mid_edge(i, other)
        return remote(src, dst, mid_send.at[i], mid_recv.at[i], partner)

    def mid_own(i):
        src, dst = mid_edge(i, core)
        return pltpu.make_async_copy(src, dst, mid_self.at[i])

    def beside(side):
        return (2 * pair, l + 1) if side == 0 else (2 * pair + 1, l - 1)

    def edge_out(i, side):
        t, j = (2 * tiles - 1, 2) if side == 0 else (0, 0)
        return remote(factor_ref.at[i, t, j], edge_raw.at[2 * core + i, side],
                      edge_send.at[i, side], edge_recv.at[2 * core + i], beside(side))

    def edge_in(k):
        return remote(edge_raw.at[k, core], edge_raw.at[k, core],
                      edge_send.at[0, 0], edge_recv.at[k], partner)

    def strip_cut(ref, target):
        return ref.at[..., pl.ds(pl.multiple_of(target * (tiles - 1) * tile, tile), cells + tile)]

    def strip_slot(ref, target):
        return ref.at[core, ..., pl.ds(pl.multiple_of((1 - target) * tile, tile), cells + tile)]

    inputs = ((rhs_hbm, rhs), (couple_hbm, couple))

    def strip_out(n):
        src, dst = inputs[n]
        return remote(strip_cut(src, other), strip_slot(dst, other), strip_send.at[n], strip_recv.at[n], partner)

    def strip_own(n):
        src, dst = inputs[n]
        return pltpu.make_async_copy(strip_cut(src, core), strip_slot(dst, core), self_sem.at[n])

    def halo_out(n, side):
        src, dst = inputs[n]
        cut = pl.ds((2 * tiles - 1) * tile, tile) if side == 0 else pl.ds(0, tile)
        slot = pl.ds(0, tile) if side == 0 else pl.ds(cells + tile, tile)
        return remote(src.at[..., cut], dst.at[core, ..., slot],
                      halo_send.at[n, side], halo_recv.at[n, core], beside(side))

    def halo_in(n, owner):
        dst = inputs[n][1]
        slot = dst.at[owner, ..., pl.ds(pl.multiple_of(core * (cells + tile), tile), tile)]
        return remote(slot, slot, halo_send.at[n, 0], halo_recv.at[n, owner], partner)

    sends = (l < lat_count - 1, l > 0)
    outer = ((core == 0) & (l > 0)) | ((core == 1) & (l < lat_count - 1))

    small = [pltpu.make_async_copy(cell_hbm, cell_ref, small_sem.at[0]),
             pltpu.make_async_copy(layer_hbm, layer_ref, small_sem.at[1])]
    for copy in small:
        copy.start()
    for n in range(2):
        strip_own(n).start()
    for i in range(2):
        mid_own(i).start()
    for i in range(2):
        for t in range(tiles):
            load(i, t).start()

    for ref in (main_in, left_in, right_in, side_left, side_right, extra_left, extra_right):
        ref[...] = jnp.zeros_like(ref)

    @pl.when(jnp.logical_not(has_left))
    def _():
        edge_raw[:, 0] = jnp.zeros_like(edge_raw[:, 0])
        rhs[..., pl.ds(0, tile)] = jnp.zeros((2, 2, 2, shots, tile), F32)
        couple[..., pl.ds(0, tile)] = jnp.zeros((2, 2, 2, 2, tile), F32)

    @pl.when(jnp.logical_not(has_right))
    def _():
        edge_raw[:, 1] = jnp.zeros_like(edge_raw[:, 1])
        rhs[..., pl.ds(cells + tile, tile)] = jnp.zeros((2, 2, 2, shots, tile), F32)
        couple[..., pl.ds(cells + tile, tile)] = jnp.zeros((2, 2, 2, 2, tile), F32)

    barrier = pltpu.get_barrier_semaphore()
    steps = [(a, b) for a in (-1, 0, 1) for b in (-1, 0, 1) if (a, b) != (0, 0)] + [(0, -2), (0, 2)]
    peers = 0
    for a, b in steps:
        there = (pair + a >= 0) & (pair + a < pairs) & (half + b >= 0) & (half + b < halves)
        peers = peers + there.astype(jnp.int32)

        @pl.when(there)
        def _():
            pl.semaphore_signal(barrier, inc=1, device_id=place(a, b), device_id_type=MESH)
    pl.semaphore_wait(barrier, peers)

    for n in range(2):
        strip_out(n).start()
    for side in range(2):
        @pl.when(sends[side])
        def _():
            for n in range(2):
                halo_out(n, side).start()
    for i in (1, 0):
        mid_out(i).start()
        for side in range(2):
            @pl.when(sends[side])
            def _():
                edge_out(i, side).start()
    for i in range(2):
        for t in range(tiles):
            part_out(i, t).start()

    def convert(k):
        owner, i = k // 2, k % 2

        def step(t, carry):
            @pl.when(core == owner)
            def _():
                load(i, t).wait()

            @pl.when(core != owner)
            def _():
                remote(raw.at[k, t], raw.at[k, t], part_send.at[i, t], part_recv.at[i, t], partner).wait_recv()
            for j in range(3):
                for c in range(2):
                    high, low = split(raw[k, t, j, c])
                    weights[k, t, pl.ds(j * tile, tile), pl.ds(c * tile, tile)] = high
                    weights[k, t, pl.ds((3 + j) * tile, tile), pl.ds(c * tile, tile)] = low
            return carry
        lax.fori_loop(0, tiles, step, 0)

    def convert_edge(k):
        owner, i = k // 2, k % 2

        @pl.when(core == owner)
        def _():
            mid_own(i).wait()

        @pl.when(core != owner)
        def _():
            slot = edge_raw.at[k, other]
            remote(slot, slot, mid_send.at[i], mid_recv.at[i], partner).wait_recv()
        pl.when(outer)(edge_in(k).wait_recv)
        for side in range(2):
            for c in range(2):
                high, low = split(edge_raw[k, side, c])
                edge_weights[k, side, pl.ds(0, tile), pl.ds(c * tile, tile)] = high
                edge_weights[k, side, pl.ds(tile, tile), pl.ds(c * tile, tile)] = low

    convert(0)
    convert(1)
    for copy in small:
        copy.wait()
    for n in range(2):
        strip_own(n).wait()
        src, dst = inputs[n]
        slot = dst.at[other, ..., pl.ds(pl.multiple_of(other * tile, tile), cells + tile)]
        remote(slot, slot, strip_send.at[n], strip_recv.at[n], partner).wait_recv()

        @pl.when(outer)
        def _():
            for owner in range(2):
                halo_in(n, owner).wait_recv()

    row = lax.broadcasted_iota(jnp.int32, (shots, wide), 0)
    lane = lax.broadcasted_iota(jnp.int32, (shots, wide), 1) + (half * cells - tile)
    src_cell = jnp.zeros((shots, wide), jnp.int32)
    src_layer = jnp.zeros((shots, wide), jnp.int32)
    for s in range(shots):
        src_cell = jnp.where(row == s, cell_ref[s], src_cell)
        src_layer = jnp.where(row == s, layer_ref[s], src_layer)
    for k in range(4):
        hit = (src_layer == pair * 4 + k) & (src_cell == lane)
        rhs[k // 2, 0, k % 2] = rhs[k // 2, 0, k % 2] + jnp.where(hit, 4.0, 0.0).astype(F32)
    convert_edge(1)

    def put(target, at, parts):
        high, low = split(jnp.concatenate(parts, axis=0))
        target[pl.ds(0, 2 * shots), at] = high
        target[pl.ds(2 * shots, 2 * shots), at] = low

    def scaled(way, k, at, parts):
        real_coef = couple[k // 2, way, 0, k % 2:k % 2 + 1, at]
        imag_coef = couple[k // 2, way, 1, k % 2:k % 2 + 1, at]
        real_part = real_coef * parts[0] - imag_coef * parts[1]
        imag_part = real_coef * parts[1] + imag_coef * parts[0]
        if way == DOWN:
            real_part = rhs[k // 2, 0, k % 2, :, at] + real_part
            imag_part = rhs[k // 2, 1, k % 2, :, at] + imag_part
        return real_part, imag_part

    def product(value, right_side):
        both = jnp.dot(jnp.concatenate([value, value], axis=1), right_side, preferred_element_type=F32)
        both = both[: 2 * shots] + both[2 * shots:]
        return (both[:shots, :tile] - both[shots:, tile:], both[:shots, tile:] + both[shots:, :tile])

    def row_block(from_ref, k, t):
        return product(from_ref[:, pl.ds(t * tile, 3 * tile)], weights[k, t])

    def arrived(main, low, high, block):
        at = pl.ds(block * tile, tile)
        parts = []
        for c in range(2):
            value = main[c, :, at]
            if block < 2:
                value = value + low[c, :, at]
            if block >= tiles:
                value = value + high[c, :, pl.ds((block - tiles) * tile, tile)]
            parts.append(value)
        return parts

    blocks = tiles + 2
    chunks = [(0, blocks)]

    def span(first, last):
        return pl.ds(first * tile, (last - first) * tile)

    def side_copies(way):
        out = out_ext.at[2 * way]
        return [
            (remote(out.at[:, :, span(0, 2)], side_right.at[way], side_send.at[way, 0], side_recv.at[way, 0],
                    place(0, -1)), has_left, has_right),
            (remote(out.at[:, :, span(tiles, blocks)], side_left.at[way], side_send.at[way, 1], side_recv.at[way, 1],
                    place(0, 1)), has_right, has_left),
        ]

    def hop_copies(way):
        out = out_ext.at[2 * way + 1]
        step = 1 if way == DOWN else -1
        onward = has_below if way == DOWN else has_above
        behind = has_above if way == DOWN else has_below
        table = [
            (span(0, 2), right_in.at[way], place(step, -1), onward & has_left, behind & has_right),
            (span(tiles, blocks), left_in.at[way], place(step, 1), onward & has_right, behind & has_left),
        ]
        for first, last in chunks:
            table.append((span(first, last), main_in.at[way, :, :, span(first, last)], place(step, 0), onward, behind))
        table.append((span(blocks - 1, blocks), extra_left.at[way], place(0, 1), has_right, has_left))
        table.append((span(0, 1), extra_right.at[way], place(0, -1), has_left, has_right))
        return [
            (remote(out.at[:, :, cut], dst, hop_send.at[way, num], hop_recv.at[way, num], to), go, come)
            for num, (cut, dst, to, go, come) in enumerate(table)
        ]

    zero = jnp.zeros((4 * shots, tile), BF16)
    inner[:, pl.ds(0, tile)] = zero
    inner[:, pl.ds(cells + tile, tile)] = zero

    def column_step(stage, k, base):
        for side in range(2):
            block = 0 if side == 0 else tiles + 1
            own = pl.ds(tile, tile) if side == 0 else pl.ds(cells, tile)
            real_part, imag_part = product(inner[:, own], edge_weights[k, side])
            out_ext[stage, 0, :, pl.ds(block * tile, tile)] = real_part
            out_ext[stage, 1, :, pl.ds(block * tile, tile)] = imag_part
        way = stage // 2
        copies = side_copies(way) if stage % 2 == 0 else hop_copies(way)
        starts = {tiles - 1: (0, 1)} if stage % 2 == 0 else {tiles - 1: (0, 1), tiles - 2: (2, 3, 4)}
        for t in [0, tiles - 1] + list(range(1, tiles - 1)):
            parts = row_block(inner, k, t)
            for c in range(2):
                value = parts[c]
                if base is not None:
                    value = value + base[k, c, :, pl.ds(t * tile, tile)]
                out_ext[stage, c, :, pl.ds((t + 1) * tile, tile)] = value
            for num in starts.get(t, ()):
                copy, go, _ = copies[num]
                pl.when(go)(copy.start)

    def take(copies):
        for copy, _, come in copies:
            pl.when(come)(copy.wait_recv)

    def first_source(way, k, main, low, high, result, result_k):
        for block in range(blocks):
            at = pl.ds(block * tile, tile)
            parts = arrived(main, low, high, block)
            if result is not None and 0 < block <= tiles:
                for c in range(2):
                    result[result_k, c, :, pl.ds((block - 1) * tile, tile)] = parts[c]
            put(source, at, scaled(way, k, at, parts))

    def second_source(way, row_k, k, result, base):
        for t in range(tiles):
            at = pl.ds(t * tile, tile)
            parts = row_block(source, row_k, t)
            if base is not None:
                parts = [parts[c] + base[row_k, c, :, at] for c in range(2)]
            for c in range(2):
                result[row_k, c, :, at] = parts[c]
            to = pl.ds((t + 1) * tile, tile)
            put(inner, to, scaled(way, k, to, parts))

    def total(way, result, k):
        take(hop_copies(way)[3:])
        out = out_ext.at[2 * way + 1]
        for c in range(2):
            for t in range(tiles):
                value = out[c, :, pl.ds((t + 1) * tile, tile)]
                if t == 0:
                    value = value + extra_left[way, c]
                if t == tiles - 1:
                    value = value + extra_right[way, c]
                result[k, c, :, pl.ds(t * tile, tile)] = value

    def second_layers():
        convert(2)
        convert(3)
        convert_edge(3)

    pl.when(has_above)(second_layers)
    take(hop_copies(DOWN)[:3])
    first_source(DOWN, 0, main_in.at[DOWN], left_in.at[DOWN], right_in.at[DOWN], None, 0)
    second_source(DOWN, 0, 1, waves, None)
    column_step(0, 1, None)
    pl.when(jnp.logical_not(has_above))(second_layers)
    take(side_copies(DOWN))
    first_source(DOWN, 2, out_ext.at[0], side_left.at[DOWN], side_right.at[DOWN], waves, 1)
    second_source(DOWN, 2, 3, waves, None)
    column_step(1, 3, None)
    convert_edge(2)
    convert_edge(0)
    total(DOWN, waves, 3)

    def result_copy(n, ref):
        return remote(ref.at[pl.ds(2 * other, 2)], result_in.at[n], result_send.at[n], result_recv.at[n], partner)

    result_copy(0, waves).start()

    @pl.when(jnp.logical_not(has_below))
    def _():
        for t in range(tiles):
            at = pl.ds(t * tile, tile)
            to = pl.ds((t + 1) * tile, tile)
            parts = [waves[3, c, :, at] for c in range(2)]
            for c in range(2):
                field[3, c, :, at] = parts[c]
            put(inner, to, scaled(UP, 2, to, parts))

    @pl.when(has_below)
    def _():
        take(hop_copies(UP)[:3])
        first_source(UP, 3, main_in.at[UP], left_in.at[UP], right_in.at[UP], None, 0)
        second_source(UP, 3, 2, field, waves)

    column_step(2, 2, waves)
    take(side_copies(UP))
    first_source(UP, 1, out_ext.at[2], side_left.at[UP], side_right.at[UP], field, 2)
    second_source(UP, 1, 0, field, waves)
    column_step(3, 0, waves)
    total(UP, field, 0)
    result_copy(1, field).start()

    for n, (ref, out_ref) in enumerate(((waves, waves_ref), (field, field_ref))):
        mine = pl.ds(pl.multiple_of(core * cells, tile), cells)
        theirs = pl.ds(pl.multiple_of(other * cells, tile), cells)
        for i in range(2):
            for c in range(2):
                out_ref[c, i, :, mine] = ref[2 * core + i, c]
        result_copy(n, ref).wait_recv()
        for i in range(2):
            for c in range(2):
                out_ref[c, i, :, theirs] = result_in[n, i, c]

    for n, ref in enumerate((waves, field)):
        result_copy(n, ref).wait_send()
        strip_out(n).wait_send()
    for i in range(2):
        mid_out(i).wait_send()
        for t in range(tiles):
            part_out(i, t).wait_send()
    for side in range(2):
        @pl.when(sends[side])
        def _():
            for n in range(2):
                halo_out(n, side).wait_send()
                edge_out(n, side).wait_send()
    for way in (DOWN, UP):
        for copy, go, _ in side_copies(way) + hop_copies(way):
            pl.when(go)(copy.wait_send)


def shards(depth_count, lat_count, rhs_field, src_cell, src_layer, factor, couple):
    layers, full_tiles = factor.shape[:2]
    tile = factor.shape[-1]
    shots = rhs_field.shape[2]
    assert layers == 2 and full_tiles % 2 == 0 and depth_count % 2 == 0
    tiles = full_tiles // 2
    cells = tiles * tile
    wide = cells + 2 * tile
    vmem = pl.BlockSpec(memory_space=pltpu.VMEM)
    dma = pltpu.SemaphoreType.DMA
    return pl.pallas_call(
        functools.partial(kernel, depth_count, lat_count),
        out_shape=[jax.ShapeDtypeStruct(rhs_field.shape, F32)] * 2,
        in_specs=[pl.BlockSpec(memory_space=pltpu.HBM)] * 5,
        out_specs=[vmem, vmem],
        scratch_shapes=[
            pltpu.SMEM(src_cell.shape, jnp.int32),
            pltpu.SMEM(src_layer.shape, jnp.int32),
            pltpu.VMEM((2, 2, 2, shots, wide), F32),
            pltpu.VMEM((2, 2, 2, 2, wide), F32),
            pltpu.VMEM((4, tiles, 3, 2, tile, tile), F32),
            pltpu.VMEM((4, tiles, 6 * tile, 2 * tile), BF16),
            pltpu.VMEM((4, 2, 2, tile, tile), F32),
            pltpu.VMEM((4, 2, 2 * tile, 2 * tile), BF16),
            pltpu.VMEM((4 * shots, wide), BF16),
            pltpu.VMEM((4 * shots, wide), BF16),
            pltpu.VMEM((4, 2, shots, wide), F32),
            pltpu.VMEM((2, 2, shots, wide), F32),
            *[pltpu.VMEM((2, 2, shots, 2 * tile), F32)] * 4,
            *[pltpu.VMEM((2, 2, shots, tile), F32)] * 2,
            *[pltpu.VMEM((4, 2, shots, cells), F32)] * 2,
            pltpu.VMEM((2, 2, 2, shots, cells), F32),
            dma((2,)), dma((2,)), dma((2, tiles)), dma((2, tiles)), dma((2, tiles)),
            dma((2,)), dma((2,)), dma((2,)),
            dma((2, 2)), dma((4,)), dma((2,)), dma((2,)), dma((2, 2)), dma((2, 2)),
            dma((2, 5)), dma((2, 5)), dma((2, 2)), dma((2, 2)), dma((2,)), dma((2,)),
        ],
        compiler_params=pltpu.CompilerParams(
            collective_id=0, has_side_effects=True, vmem_limit_bytes=44 * 1024 * 1024),
        name="sweeps",
    )(*[pltpu.with_memory_space_constraint(value, pltpu.HBM)
        for value in (src_cell, src_layer, rhs_field, couple, factor)])


def solution(mesh):
    placed = (
        P(None, "depth", None, "lat"),
        P(),
        P(),
        P("depth", "lat", None, None, None, None),
        P(None, None, "depth", "lat"),
    )
    return jax.shard_map(
        functools.partial(shards, mesh.shape["depth"], mesh.shape["lat"]),
        mesh=mesh,
        in_specs=placed,
        out_specs=(P(None, "depth", None, "lat"), P(None, "depth", None, "lat")),
        check_vma=False,
    )
```
